512 devices in a mesh: section: 4 (over x_hi, core), expert: 16 (over z), tensor: 8 (over y, x_lo).
Axes of the slice: x: 4 (x_hi: 2, x_lo: 2; x = x_hi * 2 + x_lo), y: 4, z: 16, core: 2. Of those that a mesh axis runs over, the one named last changes fastest.
Arguments:
- tokens: bfloat16 [8192, 5120], P(('section', 'expert'), 'tensor'), may hold values from -6 to 6
- norm_gain: float32 [5120], P('tensor'), may hold values from 0.1 to 1.9
- router: bfloat16 [5120, 16], P('tensor'), may hold values from -0.078125 to 0.078125
- expert_ids: int32 [8192, 1], P(('section', 'expert')), may hold values from 0 to 15; in each aligned block of 128 rows (0 to 127, 128 to 255, ...) at most 16 rows name the same one
- gate_proj: bfloat16 [16, 5120, 4096], P('expert', None, ('section', 'tensor')), may hold values from -0.078125 to 0.078125
- up_proj: bfloat16 [16, 5120, 4096], P('expert', None, ('section', 'tensor')), may hold values from -0.078125 to 0.078125
- down_proj: bfloat16 [16, 4096, 5120], P('expert', 'section', 'tensor'), may hold values from -0.09375 to 0.09375
Outputs:
- moe_out: bfloat16 [8192, 5120], P(('section', 'expert'), 'tensor')
The draws below stay inside these ranges and needn't reach their ends.
Inputs may be any that keep to these rules, and one draw needn't show every extreme that they name: `expert_ids`: within each aligned block of 128 tokens (the tokens of one group of devices along section and expert) no expert is named by more than 16 tokens, a bound that some block reaches.
All inputs are finite; a program needn't handle non-finite values.
Results may differ from the reference program's by a relative error of at most 0.017.
Values may be sent and summed in bfloat16 or wider, within the bound.
No kernel may reach another device: no remote copies, remote signals or barrier semaphores. Data moves between devices by JAX's collectives and lax.ppermute only.
A program may use at most 64 MiB of HBM per device.

```python
import math
from functools import partial
import jax
import jax.numpy as jnp
import numpy as np
from jax import lax

D = 5120
HE = 4096
TOK_DEV = 128
EXPERTS = 16
CAP = 16
TOKENS = 8192


def steps_of(own_key, extent, shards, low, high):
    level = 1.0
    for position, parts in shards:
        heights = jax.random.uniform(jax.random.fold_in(jax.random.fold_in(own_key, 6), position), (parts,), jnp.float32, low / len(shards), high / len(shards))
        level = level * jnp.repeat(jnp.exp(heights), extent[position] // parts).reshape((-1,) + (1,) * (len(extent) - 1 - position))
    return level


def shared_out(rng, own, number, rows, number_of, top, limit, lean):
    order = jax.random.permutation(rng, number_of)
    heavy_load, ordinary = shares(number_of, rows * top, limit, lean, True), shares(number_of, rows * top, limit, lean, False)
    places = jnp.arange(number_of)

    def named(tallies, offset_by):
        used = int((tallies > 0).sum())
        fixed = max(1, used // 4)
        passed = fixed + (places - fixed + offset_by * (used - fixed)) % max(1, number_of - fixed)
        return jnp.zeros((number_of,), jnp.int32).at[order[jnp.where(places < fixed, places, passed)]].set(jnp.asarray(tallies, jnp.int32))

    tallies = jnp.where(number % 4 == 0, named(heavy_load, number // 4), named(ordinary, number - number // 4 - 1))
    mixed = jax.random.permutation(jax.random.fold_in(own, 3), number_of)
    donor, taker = mixed[0:number_of // 2 * 2:2], mixed[1:number_of // 2 * 2:2]
    room = jnp.minimum(tallies[donor] - 1, limit - tallies[taker]) // 2
    room = jnp.where((donor == order[0]) | (taker == order[0]) | (tallies[taker] == 0), 0, jnp.maximum(room, 0))
    passed = jax.random.randint(jax.random.fold_in(own, 4), (number_of // 2,), 0, 1 << 20) % (room + 1)
    tallies = tallies.at[donor].add(-passed).at[taker].add(passed)
    members = jnp.searchsorted(jnp.cumsum(tallies), jnp.arange(rows * top), side="right").astype(jnp.int32)
    grid = members.reshape(top, rows).T
    grid = grid[jax.random.permutation(jax.random.fold_in(own, 1), rows)]
    offset_by = jax.random.randint(jax.random.fold_in(own, 2), (rows, 1), 0, top)
    return jnp.take_along_axis(grid, (jnp.arange(top)[None, :] + offset_by) % top, axis=1)


def shares(amount, total, reach, lean, full):
    loads = [(1 << 20) // math.isqrt(standing ** lean) + 1 for standing in range(1, amount + 1)]
    largest = reach if full else min(reach, max(-(-total // amount), total * loads[0] // sum(loads)))
    least = 1 if total - largest >= amount - 1 else 0
    counts, surplus = [largest] + [least] * (amount - 1), total - largest - least * (amount - 1)
    while surplus > 0:
        free = [i for i in range(1, amount) if counts[i] < largest] or [i for i in range(1, amount) if counts[i] < reach]
        pool, left = sum([loads[i] for i in free]), surplus
        for i in free:
            more = min(reach - counts[i], max(1, left * loads[i] // pool), surplus)
            counts[i] = counts[i] + more
            surplus = surplus - more
    return np.array(counts)


def centred(rng, shape, scale, limit, split=(), kind=jnp.bfloat16):
    values = scale * jax.random.normal(rng, shape, jnp.float32)
    if split:
        values = values * steps_of(rng, shape, split, -0.22, 0.18)
    return jnp.clip(values, -limit, limit).astype(kind)


def setup_inputs(seed: int = 0) -> dict:
    key_list = jax.random.split(jax.random.key(seed), 8)
    tokens = centred(key_list[0], (TOKENS, D), 1.0, 6.0, ((0, 64), (1, 8)))
    norm_gain = jnp.clip(1.0 + 0.18 * jax.random.normal(key_list[1], (D,), jnp.float32), 0.1, 1.9)
    router = centred(key_list[2], (D, EXPERTS), D ** -0.5, 0.078125, ((0, 8),))
    expert_ids_keys = jax.random.split(jax.random.fold_in(key_list[3], 1), TOKENS // TOK_DEV)
    expert_ids_turns = jax.random.permutation(jax.random.fold_in(key_list[3], 3), TOKENS // TOK_DEV)
    expert_ids = jax.vmap(lambda own, number: shared_out(jax.random.fold_in(key_list[3], 2), own, number, TOK_DEV, EXPERTS, 1, CAP, 2))(expert_ids_keys, expert_ids_turns).reshape((TOKENS, 1))
    gate_proj = centred(key_list[4], (EXPERTS, D, HE), D ** -0.5, 0.078125, ((0, 16), (2, 32)))
    up_proj = centred(key_list[5], (EXPERTS, D, HE), D ** -0.5, 0.078125, ((0, 16), (2, 32)))
    down_proj = centred(key_list[6], (EXPERTS, HE, D), HE ** -0.5, 0.09375, ((0, 16), (1, 4), (2, 8)))
    return dict(tokens=tokens, norm_gain=norm_gain, router=router, expert_ids=expert_ids, gate_proj=gate_proj, up_proj=up_proj, down_proj=down_proj)


EPSILON = 1e-05

def slot_table(expert_ids, experts, capacity):
    chosen = expert_ids[:, 0].astype(jnp.int32)
    member = (chosen[:, None] == jnp.arange(experts, dtype=jnp.int32)[None, :]).astype(jnp.int32)
    earlier = (jnp.cumsum(member, axis=0) - member).astype(jnp.int32)
    placed = (chosen * capacity + lax.optimization_barrier(jnp.sum(earlier * member, axis=1))).astype(jnp.int32)
    placing = placed[:, None] == jnp.arange(experts * capacity, dtype=jnp.int32)[None, :]
    return (member, placing)

def normalize(tokens, norm_gain, squares):
    values = tokens.astype(jnp.float32)
    return (values * lax.rsqrt(squares / D + EPSILON) * norm_gain).astype(jnp.bfloat16)

def expert_apply(inputs):
    rows, gate_w, up_w, down_w = inputs
    gate = jnp.dot(rows, gate_w, preferred_element_type=jnp.float32)
    upper = jnp.dot(rows, up_w, preferred_element_type=jnp.float32)
    hidden = (jax.nn.silu(gate) * upper).astype(jnp.bfloat16)
    return jnp.dot(hidden, down_w, preferred_element_type=jnp.float32).astype(jnp.bfloat16)

def reference(tokens, norm_gain, router, expert_ids, gate_proj, up_proj, down_proj):
    values = tokens.astype(jnp.float32)
    normed = normalize(tokens, norm_gain, lax.optimization_barrier(jnp.sum(values * values, axis=1, keepdims=True)))
    logits = jnp.dot(normed, router, preferred_element_type=jnp.float32)
    groups = tokens.shape[0] // TOK_DEV
    member, placing = jax.vmap(partial(slot_table, experts=EXPERTS, capacity=CAP))(expert_ids.reshape(groups, TOK_DEV, 1))
    member = member.reshape(groups * TOK_DEV, EXPERTS)
    score = jax.nn.sigmoid(lax.optimization_barrier(jnp.sum(jnp.where(member > 0, logits, jnp.float32(0.0)), axis=1)))
    routed = (normed.astype(jnp.float32) * score[:, None]).astype(jnp.bfloat16)
    routed = routed.reshape(groups, TOK_DEV, D)
    placing_f = placing.astype(jnp.float32)
    buffers = jnp.einsum('gtc,gtd->gcd', placing_f, routed.astype(jnp.float32)).astype(jnp.bfloat16)
    per_expert = buffers.reshape(groups, EXPERTS, CAP, D).transpose(1, 0, 2, 3).reshape(EXPERTS, groups * CAP, D)
    outputs = lax.map(expert_apply, (per_expert, gate_proj, up_proj, down_proj))
    back = outputs.reshape(EXPERTS, groups, CAP, D).transpose(1, 0, 2, 3).reshape(groups, EXPERTS * CAP, D)
    result = jnp.einsum('gtc,gcd->gtd', placing_f, back.astype(jnp.float32))
    return result.reshape(groups * TOK_DEV, D).astype(jnp.bfloat16)
```

```python
import functools

import jax
import jax.numpy as jnp
import numpy as np
from jax import lax
from jax.experimental import pallas as pl
from jax.experimental.pallas import tpu as pltpu
from jax.sharding import Mesh, PartitionSpec as P

D = 5120
EPSILON = 1e-05
EXPERTS = 16
CAP = 16
SLOTS = EXPERTS * CAP
TOK = 128
FEAT = 640
TENSOR = 8
EXTRA = 8
VMEM = 48 * 1024 * 1024
TENSOR_AXES = ("y", "xl")


def column_of(row):
    count = row.shape[1]
    i = lax.broadcasted_iota(jnp.int32, (count, count), 0)
    j = lax.broadcasted_iota(jnp.int32, (count, count), 1)
    return jnp.sum(jnp.where(i == j, row, 0), axis=1, keepdims=True), i, j


def dispatch_kernel(ids_ref, tokens_ref, out_ref):
    row = ids_ref[...]
    col, i, j = column_of(row)
    earlier = jnp.sum(jnp.where((col == row) & (i < j), 1, 0), axis=0, keepdims=True)
    placed = row * CAP + earlier
    slot = lax.broadcasted_iota(jnp.int32, (SLOTS, TOK), 0)
    placing = (slot == placed).astype(jnp.float32).astype(jnp.bfloat16)
    out_ref[...] = jnp.dot(
        placing, tokens_ref[...], preferred_element_type=jnp.float32
    ).astype(jnp.bfloat16)


def combine_kernel(ids_ref, back_ref, out_ref):
    row = ids_ref[...]
    col, i, j = column_of(row)
    earlier = jnp.sum(jnp.where((col == row) & (j < i), 1, 0), axis=1, keepdims=True)
    placed = col * CAP + earlier
    slot = lax.broadcasted_iota(jnp.int32, (TOK, SLOTS), 1)
    placing = (slot == placed).astype(jnp.float32).astype(jnp.bfloat16)
    out_ref[...] = jnp.dot(
        placing, back_ref[...], preferred_element_type=jnp.float32
    ).astype(jnp.bfloat16)


def gained(x_ref):
    rows = x_ref[0, :SLOTS, :].astype(jnp.float32)
    more = x_ref[0, SLOTS:, :].astype(jnp.float32)
    gain = more[0:1] + more[1:2] + more[2:3]
    return rows, rows * gain, more[3:4]


def activated(acc, scale, out_ref):
    for k in range(2):
        gate = acc[:, 256 * k : 256 * k + 128] * scale
        upper = acc[:, 256 * k + 128 : 256 * k + 256] * scale
        out_ref[:, 128 * k : 128 * k + 128] = (jax.nn.silu(gate) * upper).astype(jnp.bfloat16)


def joined(refs, axis):
    return jnp.concatenate([r[...] for r in refs], axis=axis)


def first_kernel(x_ref, g0, u0, g1, u1, out_ref, scale_ref, acc, squares, logit):
    step = pl.program_id(0)

    @pl.when(step == 0)
    def _():
        acc[...] = jnp.zeros_like(acc)
        squares[...] = jnp.zeros_like(squares)
        logit[...] = jnp.zeros_like(logit)

    rows, values, router = gained(x_ref)
    squares[...] += jnp.sum(rows * rows, axis=1, keepdims=True)
    logit[...] += jnp.sum(values * router, axis=1, keepdims=True)
    acc[...] += jnp.dot(
        values.astype(jnp.bfloat16), joined((g0, u0, g1, u1), 1), preferred_element_type=jnp.float32
    )

    @pl.when(step == TENSOR - 1)
    def _():
        rstd = lax.rsqrt(squares[...] / D + EPSILON)
        scale = rstd * jax.nn.sigmoid(logit[...] * rstd)
        scale_ref[...] = scale
        activated(acc[...], scale, out_ref)


def second_kernel(x_ref, scale_ref, g0, u0, g1, u1, out_ref, acc):
    step = pl.program_id(0)

    @pl.when(step == 0)
    def _():
        acc[...] = jnp.zeros_like(acc)

    _, values, _ = gained(x_ref)
    acc[...] += jnp.dot(
        values.astype(jnp.bfloat16), joined((g0, u0, g1, u1), 1), preferred_element_type=jnp.float32
    )

    @pl.when(step == TENSOR - 1)
    def _():
        activated(acc[...], scale_ref[...], out_ref)


X_SPEC = pl.BlockSpec((1, SLOTS + EXTRA, FEAT), lambda t: (t, 0, 0))
W_SPEC = pl.BlockSpec((FEAT, 128), lambda t: (t, 0))
H_SPEC = pl.BlockSpec((SLOTS, 256), lambda t: (0, 0))
S_SPEC = pl.BlockSpec((SLOTS, 1), lambda t: (0, 0))
HIDDEN = jax.ShapeDtypeStruct((SLOTS, 256), jnp.bfloat16)
GATE_COST = pl.CostEstimate(
    flops=2 * SLOTS * D * 512, bytes_accessed=2 * (D * 512 + D * SLOTS), transcendentals=SLOTS * 256
)
DOWN_COST = pl.CostEstimate(
    flops=2 * SLOTS * 2048 * FEAT, bytes_accessed=2 * 2048 * (FEAT + SLOTS), transcendentals=0
)
PARAMS = pltpu.CompilerParams(vmem_limit_bytes=VMEM, dimension_semantics=("arbitrary",))


def first_half(x, g0, u0, g1, u1):
    return pl.pallas_call(
        first_kernel,
        grid=(TENSOR,),
        in_specs=[X_SPEC] + [W_SPEC] * 4,
        out_specs=[H_SPEC, S_SPEC],
        out_shape=[HIDDEN, jax.ShapeDtypeStruct((SLOTS, 1), jnp.float32)],
        scratch_shapes=[
            pltpu.VMEM((SLOTS, 512), jnp.float32),
            pltpu.VMEM((SLOTS, 1), jnp.float32),
            pltpu.VMEM((SLOTS, 1), jnp.float32),
        ],
        compiler_params=PARAMS,
        cost_estimate=GATE_COST,
    )(x, g0, u0, g1, u1)


def second_half(x, scale, g0, u0, g1, u1):
    return pl.pallas_call(
        second_kernel,
        grid=(TENSOR,),
        in_specs=[X_SPEC, S_SPEC] + [W_SPEC] * 4,
        out_specs=H_SPEC,
        out_shape=HIDDEN,
        scratch_shapes=[pltpu.VMEM((SLOTS, 512), jnp.float32)],
        compiler_params=PARAMS,
        cost_estimate=GATE_COST,
    )(x, scale, g0, u0, g1, u1)


def down_kernel(last, h_ref, d0, d1, *rest):
    step = pl.program_id(0)
    before, (out_ref, acc) = rest[:-2], rest[-2:]

    @pl.when(step == 0)
    def _():
        acc[...] = before[0][...] if before else jnp.zeros_like(acc)

    acc[...] += jnp.dot(h_ref[0], joined((d0, d1), 0), preferred_element_type=jnp.float32)

    @pl.when(step == TENSOR - 1)
    def _():
        out_ref[...] = acc[...].astype(out_ref.dtype)


def down_half(hidden, d0, d1, before, dtype, order):
    total = pl.BlockSpec((SLOTS, FEAT), lambda t: (0, 0))
    d_spec = pl.BlockSpec((128, FEAT), lambda t: (t, 0))
    h_spec = pl.BlockSpec((1, SLOTS, 256), lambda t: (order(t), 0, 0))
    return pl.pallas_call(
        functools.partial(down_kernel, before is not None),
        grid=(TENSOR,),
        in_specs=[h_spec, d_spec, d_spec] + ([total] if before is not None else []),
        out_specs=total,
        out_shape=jax.ShapeDtypeStruct((SLOTS, FEAT), dtype),
        scratch_shapes=[pltpu.VMEM((SLOTS, FEAT), jnp.float32)],
        compiler_params=PARAMS,
        cost_estimate=DOWN_COST,
    )(hidden, d0, d1, *(() if before is None else (before,)))


def gathered(array):
    copies = jnp.broadcast_to(array[None], (TENSOR, *array.shape))
    return lax.all_to_all(copies, TENSOR_AXES, 0, 0, tiled=True)


def over_experts(array):
    parts = array.reshape(EXPERTS, CAP, FEAT)
    return lax.all_to_all(parts, "z", 0, 0, tiled=True).reshape(SLOTS, FEAT)


def other_core(array):
    return lax.ppermute(array, "co", [(0, 1), (1, 0)])


def across_border(array):
    return lax.ppermute(array, ("xh", "xl"), [(i, 3 - i) for i in range(4)])


def across_halves(array):
    return lax.ppermute(array, "xh", [(0, 1), (1, 0)])


def side_rows(norm_gain, router):
    high = norm_gain.astype(jnp.bfloat16)
    rest = norm_gain - high.astype(jnp.float32)
    middle = rest.astype(jnp.bfloat16)
    low = (rest - middle.astype(jnp.float32)).astype(jnp.bfloat16)
    mine = lax.axis_index("z") == jnp.arange(EXPERTS, dtype=jnp.int32)
    column = jnp.sum(jnp.where(mine[None, :], router.astype(jnp.float32), 0.0), axis=1)
    zero = jnp.zeros_like(high)
    return jnp.stack([high, middle, low, column.astype(jnp.bfloat16)] + [zero] * (EXTRA - 4))


def on_device(tokens, norm_gain, router, expert_ids, gate_proj, up_proj, down_proj):
    ids = expert_ids.reshape(1, TOK)
    gate, upper, down = gate_proj[0], up_proj[0], down_proj[0]

    outgoing = pl.pallas_call(
        dispatch_kernel, out_shape=jax.ShapeDtypeStruct((SLOTS, FEAT), jnp.bfloat16)
    )(ids, tokens)
    arrived = over_experts(outgoing)

    gate_far, upper_far = across_border(gate), across_border(upper)
    gate_near, upper_near = other_core(gate), other_core(upper)
    gate_last, upper_last = other_core(gate_far), other_core(upper_far)
    down_far, down_near = across_halves(down), other_core(down)
    down_last = other_core(down_far)

    rows = gathered(jnp.concatenate([arrived, side_rows(norm_gain, router)], axis=0))
    hidden, scale = first_half(rows, gate, upper, gate_near, upper_near)
    full = gathered(hidden)
    hidden_far = second_half(rows, scale, gate_far, upper_far, gate_last, upper_last)
    full_far = gathered(hidden_far)
    part = down_half(full, down, down_near, None, jnp.float32, lambda t: t)
    summed = down_half(
        full_far, down_far, down_last, part, jnp.bfloat16, lambda t: t + 1 - 2 * (t % 2)
    )
    returned = over_experts(summed)
    return pl.pallas_call(
        combine_kernel, out_shape=jax.ShapeDtypeStruct((TOK, FEAT), jnp.bfloat16)
    )(ids, returned)


def solution(mesh):
    fine = Mesh(
        np.asarray(mesh.devices).reshape(2, 2, 16, 4, 2), ("xh", "co", "z", "y", "xl")
    )
    section, tensor = ("xh", "co"), ("y", "xl")
    in_specs = (
        P((*section, "z"), tensor),
        P(tensor),
        P(tensor, None),
        P((*section, "z"), None),
        P("z", None, (*section, *tensor)),
        P("z", None, (*section, *tensor)),
        P("z", section, tensor),
    )
    return jax.shard_map(
        on_device,
        mesh=fine,
        in_specs=in_specs,
        out_specs=P((*section, "z"), tensor),
        check_vma=False,
    )
```

```python
import functools

import jax
import jax.numpy as jnp
import numpy as np
from jax import lax
from jax.experimental import pallas as pl
from jax.experimental.pallas import tpu as pltpu
from jax.sharding import Mesh, PartitionSpec as P

D = 5120
EPSILON = 1e-05
EXPERTS = 16
CAP = 16
SLOTS = EXPERTS * CAP
TOK = 128
FEAT = 640
TENSOR = 8
EXTRA = 8
VMEM = 20 * 1024 * 1024
PIECES = 4
PER = TENSOR // PIECES
DOWN_PIECES = 2
FLIPPED = (1, 0, 3, 2, 5, 4, 7, 6)
TENSOR_AXES = ("y", "xl")


def column_of(row):
    count = row.shape[1]
    i = lax.broadcasted_iota(jnp.int32, (count, count), 0)
    j = lax.broadcasted_iota(jnp.int32, (count, count), 1)
    return jnp.sum(jnp.where(i == j, row, 0), axis=1, keepdims=True), i, j


def dispatch_kernel(ids_ref, tokens_ref, out_ref):
    row = ids_ref[...]
    col, i, j = column_of(row)
    earlier = jnp.sum(jnp.where((col == row) & (i < j), 1, 0), axis=0, keepdims=True)
    placed = row * CAP + earlier
    slot = lax.broadcasted_iota(jnp.int32, (SLOTS, TOK), 0)
    placing = (slot == placed).astype(jnp.float32).astype(jnp.bfloat16)
    out_ref[...] = jnp.dot(
        placing, tokens_ref[...], preferred_element_type=jnp.float32
    ).astype(jnp.bfloat16)


def combine_kernel(ids_ref, back_ref, out_ref):
    row = ids_ref[...]
    col, i, j = column_of(row)
    earlier = jnp.sum(jnp.where((col == row) & (j < i), 1, 0), axis=1, keepdims=True)
    placed = col * CAP + earlier
    slot = lax.broadcasted_iota(jnp.int32, (TOK, SLOTS), 1)
    placing = (slot == placed).astype(jnp.float32).astype(jnp.bfloat16)
    out_ref[...] = jnp.dot(
        placing, back_ref[...], preferred_element_type=jnp.float32
    ).astype(jnp.bfloat16)


def gained(x_ref, k):
    rows = x_ref[k, :SLOTS, :].astype(jnp.float32)
    more = x_ref[k, SLOTS:, :].astype(jnp.float32)
    return rows, rows * (more[0:1] + more[1:2] + more[2:3]), more[3:4]


def fetched(sources, held, sems, pieces):
    depth = held.shape[1] // pieces
    copies = []
    for piece in range(pieces):
        part = pl.ds(piece * depth, depth)
        for k, source in enumerate(sources):
            copies.append(
                pltpu.make_async_copy(source.at[part], held.at[k, part], sems.at[piece, k])
            )
    for copy in copies:
        copy.start()
    return lambda piece: [c.wait() for c in copies[len(sources) * piece :][: len(sources)]]


def activated(acc, scale, out_ref):
    for k in range(2):
        gate = acc[:, 256 * k : 256 * k + 128] * scale
        upper = acc[:, 256 * k + 128 : 256 * k + 256] * scale
        out_ref[:, 128 * k : 128 * k + 128] = (jax.nn.silu(gate) * upper).astype(jnp.bfloat16)


def weighed(held, piece):
    depth = PER * FEAT
    return jnp.concatenate(
        [held[k, piece * depth : (piece + 1) * depth, :] for k in range(4)], axis=1
    )


def first_kernel(x_ref, g0, u0, g1, u1, out_ref, scale_ref, held, acc, sems):
    wait = fetched((g0, u0, g1, u1), held, sems, PIECES)
    squares, logit = 0.0, 0.0
    for piece in range(PIECES):
        parts = []
        for k in range(PER):
            rows, values, router = gained(x_ref, piece * PER + k)
            squares += jnp.sum(rows * rows, axis=1, keepdims=True)
            logit += jnp.sum(values * router, axis=1, keepdims=True)
            parts.append(values.astype(jnp.bfloat16))
        wait(piece)
        term = jnp.dot(
            jnp.concatenate(parts, axis=1), weighed(held, piece), preferred_element_type=jnp.float32
        )
        acc[...] = term if piece == 0 else acc[...] + term
    rstd = lax.rsqrt(squares / D + EPSILON)
    scale = rstd * jax.nn.sigmoid(logit * rstd)
    scale_ref[...] = scale
    activated(acc, scale, out_ref)


def second_kernel(x_ref, scale_ref, g0, u0, g1, u1, out_ref, held, acc, sems):
    wait = fetched((g0, u0, g1, u1), held, sems, PIECES)
    for piece in range(PIECES):
        parts = [gained(x_ref, piece * PER + k)[1].astype(jnp.bfloat16) for k in range(PER)]
        wait(piece)
        term = jnp.dot(
            jnp.concatenate(parts, axis=1), weighed(held, piece), preferred_element_type=jnp.float32
        )
        acc[...] = term if piece == 0 else acc[...] + term
    activated(acc, scale_ref[...], out_ref)


IN_VMEM = pl.BlockSpec(memory_space=pltpu.VMEM)
IN_HBM = pl.BlockSpec(memory_space=pl.ANY)


def left_in_hbm(arrays):
    return [pltpu.with_memory_space_constraint(a, pltpu.HBM) for a in arrays]


HIDDEN = jax.ShapeDtypeStruct((SLOTS, 256), jnp.bfloat16)
GATE_COST = pl.CostEstimate(
    flops=2 * SLOTS * D * 512, bytes_accessed=2 * (D * 512 + D * SLOTS), transcendentals=SLOTS * 256
)
DOWN_COST = pl.CostEstimate(
    flops=2 * SLOTS * 2048 * FEAT, bytes_accessed=2 * 2048 * (FEAT + SLOTS), transcendentals=0
)
PARAMS = pltpu.CompilerParams(vmem_limit_bytes=VMEM)
GATE_SCRATCH = [
    pltpu.VMEM((4, D, 128), jnp.bfloat16),
    pltpu.VMEM((SLOTS, 512), jnp.float32),
    pltpu.SemaphoreType.DMA((PIECES, 4)),
]


def first_half(x, *weights):
    return pl.pallas_call(
        first_kernel,
        in_specs=[IN_VMEM] + [IN_HBM] * 4,
        out_specs=[IN_VMEM, IN_VMEM],
        out_shape=[HIDDEN, jax.ShapeDtypeStruct((SLOTS, 1), jnp.float32)],
        scratch_shapes=GATE_SCRATCH,
        compiler_params=PARAMS,
        cost_estimate=GATE_COST,
    )(x, *left_in_hbm(weights))


def second_half(x, scale, *weights):
    return pl.pallas_call(
        second_kernel,
        in_specs=[IN_VMEM, IN_VMEM] + [IN_HBM] * 4,
        out_specs=IN_VMEM,
        out_shape=HIDDEN,
        scratch_shapes=GATE_SCRATCH,
        compiler_params=PARAMS,
        cost_estimate=GATE_COST,
    )(x, scale, *left_in_hbm(weights))


def down_kernel(order, h_ref, d0, d1, *rest):
    *before, out_ref, held, acc, sems = rest
    wait = fetched((d0, d1), held, sems, DOWN_PIECES)
    each = TENSOR // DOWN_PIECES
    for piece in range(DOWN_PIECES):
        places = range(piece * each, (piece + 1) * each)
        hidden = jnp.concatenate([h_ref[order[k]] for k in places], axis=1)
        wait(piece)
        slices = [held[w, 128 * k : 128 * k + 128, :] for k in places for w in range(2)]
        term = jnp.dot(
            hidden, jnp.concatenate(slices, axis=0), preferred_element_type=jnp.float32
        )
        if piece == 0:
            acc[...] = before[0][...] + term if before else term
        elif piece < DOWN_PIECES - 1:
            acc[...] += term
        else:
            out_ref[...] = (acc[...] + term).astype(out_ref.dtype)


def down_half(hidden, d0, d1, before, dtype, order):
    return pl.pallas_call(
        functools.partial(down_kernel, order),
        in_specs=[IN_VMEM, IN_HBM, IN_HBM] + ([IN_VMEM] if before is not None else []),
        out_specs=IN_VMEM,
        out_shape=jax.ShapeDtypeStruct((SLOTS, FEAT), dtype),
        scratch_shapes=[
            pltpu.VMEM((2, 1024, FEAT), jnp.bfloat16),
            pltpu.VMEM((SLOTS, FEAT), jnp.float32),
            pltpu.SemaphoreType.DMA((DOWN_PIECES, 2)),
        ],
        compiler_params=PARAMS,
        cost_estimate=DOWN_COST,
    )(hidden, *left_in_hbm((d0, d1)), *(() if before is None else (before,)))


def gathered(array):
    copies = jnp.broadcast_to(array[None], (TENSOR, *array.shape))
    return lax.all_to_all(copies, TENSOR_AXES, 0, 0, tiled=True)


def over_experts(array):
    parts = array.reshape(EXPERTS, CAP, FEAT)
    return lax.all_to_all(parts, "z", 0, 0, tiled=True).reshape(SLOTS, FEAT)


def other_core(array):
    return lax.ppermute(array, "co", [(0, 1), (1, 0)])


def across_border(array):
    return lax.ppermute(array, ("xh", "xl"), [(i, 3 - i) for i in range(4)])


def across_halves(array):
    return lax.ppermute(array, "xh", [(0, 1), (1, 0)])


def side_rows(norm_gain, router):
    high = norm_gain.astype(jnp.bfloat16)
    rest = norm_gain - high.astype(jnp.float32)
    middle = rest.astype(jnp.bfloat16)
    low = (rest - middle.astype(jnp.float32)).astype(jnp.bfloat16)
    mine = lax.axis_index("z") == jnp.arange(EXPERTS, dtype=jnp.int32)
    column = jnp.sum(jnp.where(mine[None, :], router.astype(jnp.float32), 0.0), axis=1)
    zero = jnp.zeros_like(high)
    return jnp.stack([high, middle, low, column.astype(jnp.bfloat16)] + [zero] * (EXTRA - 4))


def on_device(tokens, norm_gain, router, expert_ids, gate_proj, up_proj, down_proj):
    ids = expert_ids.reshape(1, TOK)
    gate, upper, down = gate_proj[0], up_proj[0], down_proj[0]

    outgoing = pl.pallas_call(
        dispatch_kernel, out_shape=jax.ShapeDtypeStruct((SLOTS, FEAT), jnp.bfloat16)
    )(ids, tokens)
    arrived = over_experts(outgoing)

    gate_far, upper_far = across_border(gate), across_border(upper)
    gate_near, upper_near = other_core(gate), other_core(upper)
    arrived, gate_far = lax.optimization_barrier((arrived, gate_far))
    gate_last, upper_last = other_core(gate_far), other_core(upper_far)
    down_near = other_core(down)
    down_sent, upper_far = lax.optimization_barrier((down, upper_far))
    down_far = across_halves(down_sent)
    down_last = other_core(down_far)

    rows = gathered(jnp.concatenate([arrived, side_rows(norm_gain, router)], axis=0))
    hidden, scale = first_half(rows, gate, upper, gate_near, upper_near)
    full = gathered(hidden)
    hidden_far = second_half(rows, scale, gate_far, upper_far, gate_last, upper_last)
    full_far = gathered(hidden_far)
    part = down_half(full, down, down_near, None, jnp.float32, tuple(range(TENSOR)))
    summed = down_half(full_far, down_far, down_last, part, jnp.bfloat16, FLIPPED)
    returned = over_experts(summed)
    return pl.pallas_call(
        combine_kernel, out_shape=jax.ShapeDtypeStruct((TOK, FEAT), jnp.bfloat16)
    )(ids, returned)


def solution(mesh):
    fine = Mesh(
        np.asarray(mesh.devices).reshape(2, 2, 16, 4, 2), ("xh", "co", "z", "y", "xl")
    )
    section, tensor = ("xh", "co"), ("y", "xl")
    in_specs = (
        P((*section, "z"), tensor),
        P(tensor),
        P(tensor, None),
        P((*section, "z"), None),
        P("z", None, (*section, *tensor)),
        P("z", None, (*section, *tensor)),
        P("z", section, tensor),
    )
    return jax.shard_map(
        on_device,
        mesh=fine,
        in_specs=in_specs,
        out_specs=P((*section, "z"), tensor),
        check_vma=False,
    )
```

```python
import jax
import jax.numpy as jnp
import numpy as np
from jax import lax
from jax.experimental import pallas as pl
from jax.experimental.pallas import tpu as pltpu
from jax.sharding import Mesh, PartitionSpec as P

D = 5120
EPSILON = 1e-05
EXPERTS = 16
CAP = 16
SLOTS = EXPERTS * CAP
TOK = 128
FEAT = 640
TENSOR = 8
EXTRA = 8
VMEM = 28 * 1024 * 1024
PIECES = 4
PER = TENSOR // PIECES
DOWN_PIECES = 4
TOP = D // PIECES
TENSOR_AXES = ("y", "xl")


def column_of(row):
    count = row.shape[1]
    i = lax.broadcasted_iota(jnp.int32, (count, count), 0)
    j = lax.broadcasted_iota(jnp.int32, (count, count), 1)
    return jnp.sum(jnp.where(i == j, row, 0), axis=1, keepdims=True), i, j


def dispatch_kernel(ids_ref, tokens_ref, out_ref):
    row = ids_ref[...]
    col, i, j = column_of(row)
    earlier = jnp.sum(jnp.where((col == row) & (i < j), 1, 0), axis=0, keepdims=True)
    placed = row * CAP + earlier
    slot = lax.broadcasted_iota(jnp.int32, (SLOTS, TOK), 0)
    placing = (slot == placed).astype(jnp.float32).astype(jnp.bfloat16)
    out_ref[...] = jnp.dot(
        placing, tokens_ref[...], preferred_element_type=jnp.float32
    ).astype(jnp.bfloat16)


def combine_kernel(ids_ref, back_ref, out_ref):
    row = ids_ref[...]
    col, i, j = column_of(row)
    earlier = jnp.sum(jnp.where((col == row) & (j < i), 1, 0), axis=1, keepdims=True)
    placed = col * CAP + earlier
    slot = lax.broadcasted_iota(jnp.int32, (TOK, SLOTS), 1)
    placing = (slot == placed).astype(jnp.float32).astype(jnp.bfloat16)
    out_ref[...] = jnp.dot(
        placing, back_ref[...], preferred_element_type=jnp.float32
    ).astype(jnp.bfloat16)


def gained(x_ref, k):
    rows = x_ref[k, :SLOTS, :].astype(jnp.float32)
    more = x_ref[k, SLOTS:, :].astype(jnp.float32)
    return rows, rows * (more[0:1] + more[1:2] + more[2:3]), more[3:4]


def fetched(sources, held, sems, pieces):
    depth = held.shape[1] // pieces
    copies = []
    for piece in range(pieces):
        for k, parts in enumerate(sources):
            start, index = piece * depth, 0
            while start >= parts[index].shape[0]:
                start, index = start - parts[index].shape[0], index + 1
            copies.append(
                pltpu.make_async_copy(
                    parts[index].at[pl.ds(start, depth)],
                    held.at[k, pl.ds(piece * depth, depth)],
                    sems.at[piece, k],
                )
            )
    for copy in copies:
        copy.start()
    return lambda piece: [c.wait() for c in copies[len(sources) * piece :][: len(sources)]]


def weighed(held, piece):
    depth = PER * FEAT
    return jnp.concatenate(
        [held[k, piece * depth : (piece + 1) * depth, :] for k in range(8)], axis=1
    )


def hidden_kernel(x_ref, g0, u0, g1, u1, g2, u2, v2, g3, u3, v3, out_ref, held, acc, sems):
    weights = ((g0,), (u0,), (g1,), (u1,), (g2,), (u2, v2), (g3,), (u3, v3))
    wait = fetched(weights, held, sems, PIECES)
    squares, logit = 0.0, 0.0
    for piece in range(PIECES):
        parts = []
        for k in range(PER):
            rows, values, router = gained(x_ref, piece * PER + k)
            squares += jnp.sum(rows * rows, axis=1, keepdims=True)
            logit += jnp.sum(values * router, axis=1, keepdims=True)
            parts.append(values.astype(jnp.bfloat16))
        wait(piece)
        term = jnp.dot(
            jnp.concatenate(parts, axis=1), weighed(held, piece), preferred_element_type=jnp.float32
        )
        acc[...] = term if piece == 0 else acc[...] + term
    rstd = lax.rsqrt(squares / D + EPSILON)
    scale = rstd * jax.nn.sigmoid(logit * rstd)
    for k in range(4):
        gate = acc[:, 256 * k : 256 * k + 128] * scale
        upper = acc[:, 256 * k + 128 : 256 * k + 256] * scale
        out_ref[:, 128 * k : 128 * k + 128] = (jax.nn.silu(gate) * upper).astype(jnp.bfloat16)


def down_kernel(h_ref, d0, d1, d2, d3, out_ref, held, acc, sems):
    wait = fetched(((d0,), (d1,), (d2,), (d3,)), held, sems, DOWN_PIECES)
    each = TENSOR // DOWN_PIECES
    for piece in range(DOWN_PIECES):
        places = range(piece * each, (piece + 1) * each)
        hidden = jnp.concatenate(
            [h for k in places for h in (h_ref[k, :, :256], h_ref[k ^ 1, :, 256:])], axis=1
        )
        wait(piece)
        slices = [held[w, 128 * k : 128 * k + 128, :] for k in places for w in range(4)]
        term = jnp.dot(
            hidden, jnp.concatenate(slices, axis=0), preferred_element_type=jnp.float32
        )
        if piece == 0:
            acc[...] = term
        elif piece < DOWN_PIECES - 1:
            acc[...] += term
        else:
            out_ref[...] = (acc[...] + term).astype(out_ref.dtype)


IN_VMEM = pl.BlockSpec(memory_space=pltpu.VMEM)
IN_HBM = pl.BlockSpec(memory_space=pl.ANY)
PARAMS = pltpu.CompilerParams(vmem_limit_bytes=VMEM)


def left_in_hbm(arrays):
    return [pltpu.with_memory_space_constraint(a, pltpu.HBM) for a in arrays]


def hidden_units(x, *weights):
    return pl.pallas_call(
        hidden_kernel,
        in_specs=[IN_VMEM] + [IN_HBM] * len(weights),
        out_specs=IN_VMEM,
        out_shape=jax.ShapeDtypeStruct((SLOTS, 512), jnp.bfloat16),
        scratch_shapes=[
            pltpu.VMEM((8, D, 128), jnp.bfloat16),
            pltpu.VMEM((SLOTS, 1024), jnp.float32),
            pltpu.SemaphoreType.DMA((PIECES, 8)),
        ],
        compiler_params=PARAMS,
        cost_estimate=pl.CostEstimate(
            flops=2 * SLOTS * D * 1024,
            bytes_accessed=2 * D * (1024 + SLOTS),
            transcendentals=SLOTS * 512,
        ),
    )(x, *left_in_hbm(weights))


def down_sums(hidden, *weights):
    return pl.pallas_call(
        down_kernel,
        in_specs=[IN_VMEM] + [IN_HBM] * 4,
        out_specs=IN_VMEM,
        out_shape=jax.ShapeDtypeStruct((SLOTS, FEAT), jnp.bfloat16),
        scratch_shapes=[
            pltpu.VMEM((4, 1024, FEAT), jnp.bfloat16),
            pltpu.VMEM((SLOTS, FEAT), jnp.float32),
            pltpu.SemaphoreType.DMA((DOWN_PIECES, 4)),
        ],
        compiler_params=PARAMS,
        cost_estimate=pl.CostEstimate(
            flops=2 * SLOTS * 4096 * FEAT,
            bytes_accessed=2 * 4096 * (FEAT + SLOTS),
            transcendentals=0,
        ),
    )(hidden, *left_in_hbm(weights))


def gathered(array):
    copies = jnp.broadcast_to(array[None], (TENSOR, *array.shape))
    return lax.all_to_all(copies, TENSOR_AXES, 0, 0, tiled=True)


def over_experts(array):
    parts = array.reshape(EXPERTS, CAP, FEAT)
    return lax.all_to_all(parts, "z", 0, 0, tiled=True).reshape(SLOTS, FEAT)


def other_core(array):
    return lax.ppermute(array, "co", [(0, 1), (1, 0)])


def across_border(array):
    return lax.ppermute(array, ("xh", "xl"), [(i, 3 - i) for i in range(4)])


def across_halves(array):
    return lax.ppermute(array, "xh", [(0, 1), (1, 0)])


def tied(*arrays):
    return lax.optimization_barrier(arrays)


def side_rows(norm_gain, router):
    high = norm_gain.astype(jnp.bfloat16)
    rest = norm_gain - high.astype(jnp.float32)
    middle = rest.astype(jnp.bfloat16)
    low = (rest - middle.astype(jnp.float32)).astype(jnp.bfloat16)
    mine = lax.axis_index("z") == jnp.arange(EXPERTS, dtype=jnp.int32)
    column = jnp.sum(jnp.where(mine[None, :], router.astype(jnp.float32), 0.0), axis=1)
    zero = jnp.zeros_like(high)
    return jnp.stack([high, middle, low, column.astype(jnp.bfloat16)] + [zero] * (EXTRA - 4))


def on_device(tokens, norm_gain, router, expert_ids, gate_proj, up_proj, down_proj):
    ids = expert_ids.reshape(1, TOK)
    gate, upper, down = gate_proj[0], up_proj[0], down_proj[0]

    outgoing = pl.pallas_call(
        dispatch_kernel, out_shape=jax.ShapeDtypeStruct((SLOTS, FEAT), jnp.bfloat16)
    )(ids, tokens)
    arrived = over_experts(outgoing)
    side = side_rows(norm_gain, router)

    gate_far = across_border(gate)
    top_sent, side = tied(upper[:TOP], side)
    top_far = across_border(top_sent)
    arrived, gate_far, top_far = tied(arrived, gate_far, top_far)
    rest_far = across_border(upper[TOP:])
    rest_far, down_sent = tied(rest_far, down)
    near = (other_core(gate), other_core(upper))
    last = (other_core(gate_far), other_core(top_far), other_core(rest_far))

    rows = gathered(jnp.concatenate([arrived, side], axis=0))
    hidden = hidden_units(rows, gate, upper, *near, gate_far, top_far, rest_far, *last)

    down_far = across_halves(down_sent)
    down_near, down_last = other_core(down), other_core(down_far)
    summed = down_sums(gathered(hidden), down, down_near, down_far, down_last)
    returned = over_experts(summed)
    return pl.pallas_call(
        combine_kernel, out_shape=jax.ShapeDtypeStruct((TOK, FEAT), jnp.bfloat16)
    )(ids, returned)


def solution(mesh):
    fine = Mesh(
        np.asarray(mesh.devices).reshape(2, 2, 16, 4, 2), ("xh", "co", "z", "y", "xl")
    )
    section, tensor = ("xh", "co"), ("y", "xl")
    in_specs = (
        P((*section, "z"), tensor),
        P(tensor),
        P(tensor, None),
        P((*section, "z"), None),
        P("z", None, (*section, *tensor)),
        P("z", None, (*section, *tensor)),
        P("z", section, tensor),
    )
    return jax.shard_map(
        on_device,
        mesh=fine,
        in_specs=in_specs,
        out_specs=P((*section, "z"), tensor),
        check_vma=False,
    )
```

```python
import jax
import jax.numpy as jnp
import numpy as np
from jax import lax
from jax.experimental import pallas as pl
from jax.experimental.pallas import tpu as pltpu
from jax.sharding import Mesh, PartitionSpec as P

D = 5120
EPSILON = 1e-05
EXPERTS = 16
CAP = 16
SLOTS = EXPERTS * CAP
TOK = 128
FEAT = 640
TENSOR = 8
EXTRA = 8
VMEM = 28 * 1024 * 1024
PIECES = 4
PER = TENSOR // PIECES
DOWN_PIECES = 4
TENSOR_AXES = ("y", "xl")


def column_of(row):
    count = row.shape[1]
    i = lax.broadcasted_iota(jnp.int32, (count, count), 0)
    j = lax.broadcasted_iota(jnp.int32, (count, count), 1)
    return jnp.sum(jnp.where(i == j, row, 0), axis=1, keepdims=True), i, j


def dispatch_kernel(ids_ref, tokens_ref, gate_ref, upper_ref, out_ref, own_ref, sems):
    copies = [
        pltpu.make_async_copy(ref, own_ref.at[k], sems.at[k])
        for k, ref in enumerate((gate_ref, upper_ref))
    ]
    for copy in copies:
        copy.start()
    row = ids_ref[...]
    col, i, j = column_of(row)
    earlier = jnp.sum(jnp.where((col == row) & (i < j), 1, 0), axis=0, keepdims=True)
    placed = row * CAP + earlier
    slot = lax.broadcasted_iota(jnp.int32, (SLOTS, TOK), 0)
    placing = (slot == placed).astype(jnp.float32).astype(jnp.bfloat16)
    out_ref[...] = jnp.dot(
        placing, tokens_ref[...], preferred_element_type=jnp.float32
    ).astype(jnp.bfloat16)
    for copy in copies:
        copy.wait()


def combine_kernel(ids_ref, back_ref, out_ref):
    row = ids_ref[...]
    col, i, j = column_of(row)
    earlier = jnp.sum(jnp.where((col == row) & (j < i), 1, 0), axis=1, keepdims=True)
    placed = col * CAP + earlier
    slot = lax.broadcasted_iota(jnp.int32, (TOK, SLOTS), 1)
    placing = (slot == placed).astype(jnp.float32).astype(jnp.bfloat16)
    out_ref[...] = jnp.dot(
        placing, back_ref[...], preferred_element_type=jnp.float32
    ).astype(jnp.bfloat16)


def gained(x_ref, k):
    rows = x_ref[k, :SLOTS, :].astype(jnp.float32)
    more = x_ref[k, SLOTS:, :].astype(jnp.float32)
    return rows, rows * (more[0:1] + more[1:2] + more[2:3]), more[3:4]


def fetched(sources, held, sems, pieces):
    depth = held.shape[1] // pieces
    copies = []
    for piece in range(pieces):
        part = pl.ds(piece * depth, depth)
        for k, source in enumerate(sources):
            copies.append(
                pltpu.make_async_copy(source.at[part], held.at[k, part], sems.at[piece, k])
            )
    for copy in copies:
        copy.start()
    return lambda piece: [c.wait() for c in copies[len(sources) * piece :][: len(sources)]]


def weighed(held, piece):
    depth = PER * FEAT
    return jnp.concatenate(
        [held[k, piece * depth : (piece + 1) * depth, :] for k in range(8)], axis=1
    )


def hidden_kernel(x_ref, own, near, far, *rest):
    *last, out_ref, held, acc, sems = rest
    weights = [pair.at[k] for pair in (own, near, far) for k in range(2)] + last
    wait = fetched(weights, held, sems, PIECES)
    squares, logit = 0.0, 0.0
    for piece in range(PIECES):
        parts = []
        for k in range(PER):
            rows, values, router = gained(x_ref, piece * PER + k)
            squares += jnp.sum(rows * rows, axis=1, keepdims=True)
            logit += jnp.sum(values * router, axis=1, keepdims=True)
            parts.append(values.astype(jnp.bfloat16))
        wait(piece)
        term = jnp.dot(
            jnp.concatenate(parts, axis=1), weighed(held, piece), preferred_element_type=jnp.float32
        )
        acc[...] = term if piece == 0 else acc[...] + term
    rstd = lax.rsqrt(squares / D + EPSILON)
    scale = rstd * jax.nn.sigmoid(logit * rstd)
    for k in range(4):
        gate = acc[:, 256 * k : 256 * k + 128] * scale
        upper = acc[:, 256 * k + 128 : 256 * k + 256] * scale
        out_ref[:, 128 * k : 128 * k + 128] = (jax.nn.silu(gate) * upper).astype(jnp.bfloat16)


def down_kernel(h_ref, d0, d1, d2, d3, out_ref, held, acc, sems):
    wait = fetched((d0, d1, d2, d3), held, sems, DOWN_PIECES)
    each = TENSOR // DOWN_PIECES
    for piece in range(DOWN_PIECES):
        places = range(piece * each, (piece + 1) * each)
        hidden = jnp.concatenate(
            [h for k in places for h in (h_ref[k, :, :256], h_ref[k ^ 1, :, 256:])], axis=1
        )
        wait(piece)
        slices = [held[w, 128 * k : 128 * k + 128, :] for k in places for w in range(4)]
        term = jnp.dot(
            hidden, jnp.concatenate(slices, axis=0), preferred_element_type=jnp.float32
        )
        if piece == 0:
            acc[...] = term
        elif piece < DOWN_PIECES - 1:
            acc[...] += term
        else:
            out_ref[...] = (acc[...] + term).astype(out_ref.dtype)


IN_VMEM = pl.BlockSpec(memory_space=pltpu.VMEM)
IN_HBM = pl.BlockSpec(memory_space=pl.ANY)
PARAMS = pltpu.CompilerParams(vmem_limit_bytes=VMEM)


def left_in_hbm(arrays):
    return [pltpu.with_memory_space_constraint(a, pltpu.HBM) for a in arrays]


def dispatched(ids, tokens, gate, upper):
    return pl.pallas_call(
        dispatch_kernel,
        in_specs=[IN_VMEM, IN_VMEM, IN_HBM, IN_HBM],
        out_specs=[IN_VMEM, IN_HBM],
        out_shape=[
            jax.ShapeDtypeStruct((SLOTS, FEAT), jnp.bfloat16),
            jax.ShapeDtypeStruct((2, D, 128), jnp.bfloat16),
        ],
        scratch_shapes=[pltpu.SemaphoreType.DMA((2,))],
    )(ids, tokens, *left_in_hbm((gate, upper)))


def hidden_units(x, *weights):
    return pl.pallas_call(
        hidden_kernel,
        in_specs=[IN_VMEM] + [IN_HBM] * len(weights),
        out_specs=IN_VMEM,
        out_shape=jax.ShapeDtypeStruct((SLOTS, 512), jnp.bfloat16),
        scratch_shapes=[
            pltpu.VMEM((8, D, 128), jnp.bfloat16),
            pltpu.VMEM((SLOTS, 1024), jnp.float32),
            pltpu.SemaphoreType.DMA((PIECES, 8)),
        ],
        compiler_params=PARAMS,
        cost_estimate=pl.CostEstimate(
            flops=2 * SLOTS * D * 1024,
            bytes_accessed=2 * D * (1024 + SLOTS),
            transcendentals=SLOTS * 512,
        ),
    )(x, *left_in_hbm(weights))


def down_sums(hidden, *weights):
    return pl.pallas_call(
        down_kernel,
        in_specs=[IN_VMEM] + [IN_HBM] * 4,
        out_specs=IN_VMEM,
        out_shape=jax.ShapeDtypeStruct((SLOTS, FEAT), jnp.bfloat16),
        scratch_shapes=[
            pltpu.VMEM((4, 1024, FEAT), jnp.bfloat16),
            pltpu.VMEM((SLOTS, FEAT), jnp.float32),
            pltpu.SemaphoreType.DMA((DOWN_PIECES, 4)),
        ],
        compiler_params=PARAMS,
        cost_estimate=pl.CostEstimate(
            flops=2 * SLOTS * 4096 * FEAT,
            bytes_accessed=2 * 4096 * (FEAT + SLOTS),
            transcendentals=0,
        ),
    )(hidden, *left_in_hbm(weights))


def gathered(array):
    copies = jnp.broadcast_to(array[None], (TENSOR, *array.shape))
    return lax.all_to_all(copies, TENSOR_AXES, 0, 0, tiled=True)


def over_experts(array):
    parts = array.reshape(EXPERTS, CAP, FEAT)
    return lax.all_to_all(parts, "z", 0, 0, tiled=True).reshape(SLOTS, FEAT)


def other_core(array):
    return lax.ppermute(array, "co", [(0, 1), (1, 0)])


def across_border(array):
    return lax.ppermute(array, ("xh", "xl"), [(i, 3 - i) for i in range(4)])


def across_halves(array):
    return lax.ppermute(array, "xh", [(0, 1), (1, 0)])


def tied(*arrays):
    return lax.optimization_barrier(arrays)


def side_rows(norm_gain, router):
    high = norm_gain.astype(jnp.bfloat16)
    rest = norm_gain - high.astype(jnp.float32)
    middle = rest.astype(jnp.bfloat16)
    low = (rest - middle.astype(jnp.float32)).astype(jnp.bfloat16)
    mine = lax.axis_index("z") == jnp.arange(EXPERTS, dtype=jnp.int32)
    column = jnp.sum(jnp.where(mine[None, :], router.astype(jnp.float32), 0.0), axis=1)
    zero = jnp.zeros_like(high)
    return jnp.stack([high, middle, low, column.astype(jnp.bfloat16)] + [zero] * (EXTRA - 4))


def on_device(tokens, norm_gain, router, expert_ids, gate_proj, up_proj, down_proj):
    ids = expert_ids.reshape(1, TOK)
    gate, upper, down = gate_proj[0], up_proj[0], down_proj[0]

    outgoing, own = dispatched(ids, tokens, gate, upper)
    arrived, token = tied(over_experts(outgoing), ids)
    side = side_rows(norm_gain, router)

    near = other_core(own)
    far, down_sent, token = tied(across_border(own), down, token)
    last = [other_core(far[k]) for k in range(2)]

    rows = gathered(jnp.concatenate([arrived, side], axis=0))
    hidden = hidden_units(rows, own, near, far, *last)

    down_far = across_halves(down_sent)
    down_near, down_last = other_core(down), other_core(down_far)
    summed = down_sums(gathered(hidden), down, down_near, down_far, down_last)
    returned = over_experts(summed)
    return pl.pallas_call(
        combine_kernel, out_shape=jax.ShapeDtypeStruct((TOK, FEAT), jnp.bfloat16)
    )(token, returned)


def solution(mesh):
    fine = Mesh(
        np.asarray(mesh.devices).reshape(2, 2, 16, 4, 2), ("xh", "co", "z", "y", "xl")
    )
    section, tensor = ("xh", "co"), ("y", "xl")
    in_specs = (
        P((*section, "z"), tensor),
        P(tensor),
        P(tensor, None),
        P((*section, "z"), None),
        P("z", None, (*section, *tensor)),
        P("z", None, (*section, *tensor)),
        P("z", section, tensor),
    )
    return jax.shard_map(
        on_device,
        mesh=fine,
        in_specs=in_specs,
        out_specs=P((*section, "z"), tensor),
        check_vma=False,
    )
```

```python
import jax
import jax.numpy as jnp
import numpy as np
from jax import lax
from jax.experimental import pallas as pl
from jax.experimental.pallas import tpu as pltpu
from jax.sharding import Mesh, PartitionSpec as P

D = 5120
EPSILON = 1e-05
EXPERTS = 16
CAP = 16
SLOTS = EXPERTS * CAP
TOK = 128
FEAT = 640
TENSOR = 8
EXTRA = 8
VMEM = 28 * 1024 * 1024
PIECES = 4
STAGES = 4
PER = TENSOR // PIECES
DOWN_PIECES = 4
TENSOR_AXES = ("y", "xl")


def column_of(row):
    count = row.shape[1]
    i = lax.broadcasted_iota(jnp.int32, (count, count), 0)
    j = lax.broadcasted_iota(jnp.int32, (count, count), 1)
    return jnp.sum(jnp.where(i == j, row, 0), axis=1, keepdims=True), i, j


def dispatch_kernel(ids_ref, tokens_ref, gate_ref, upper_ref, out_ref, own_ref, held, sems):
    depth = D // STAGES
    inward, outward = [], []
    for stage in range(STAGES):
        part = pl.ds(stage * depth, depth)
        for k, ref in enumerate((gate_ref, upper_ref)):
            inward.append(
                pltpu.make_async_copy(ref.at[part], held.at[k, part], sems.at[0, stage, k])
            )
            outward.append(
                pltpu.make_async_copy(held.at[k, part], own_ref.at[k, part], sems.at[1, stage, k])
            )
    for copy in inward:
        copy.start()
    row = ids_ref[...]
    col, i, j = column_of(row)
    earlier = jnp.sum(jnp.where((col == row) & (i < j), 1, 0), axis=0, keepdims=True)
    placed = row * CAP + earlier
    slot = lax.broadcasted_iota(jnp.int32, (SLOTS, TOK), 0)
    placing = (slot == placed).astype(jnp.float32).astype(jnp.bfloat16)
    for first, second in zip(inward, outward):
        first.wait()
        second.start()
    out_ref[...] = jnp.dot(
        placing, tokens_ref[...], preferred_element_type=jnp.float32
    ).astype(jnp.bfloat16)
    for copy in outward:
        copy.wait()


def combine_kernel(ids_ref, back_ref, out_ref):
    row = ids_ref[...]
    col, i, j = column_of(row)
    earlier = jnp.sum(jnp.where((col == row) & (j < i), 1, 0), axis=1, keepdims=True)
    placed = col * CAP + earlier
    slot = lax.broadcasted_iota(jnp.int32, (TOK, SLOTS), 1)
    placing = (slot == placed).astype(jnp.float32).astype(jnp.bfloat16)
    out_ref[...] = jnp.dot(
        placing, back_ref[...], preferred_element_type=jnp.float32
    ).astype(jnp.bfloat16)


def gained(x_ref, k):
    rows = x_ref[k, :SLOTS, :].astype(jnp.float32)
    more = x_ref[k, SLOTS:, :].astype(jnp.float32)
    return rows, rows * (more[0:1] + more[1:2] + more[2:3]), more[3:4]


def fetched(sources, held, sems, pieces):
    depth = held.shape[1] // pieces
    copies = []
    for piece in range(pieces):
        part = pl.ds(piece * depth, depth)
        for k, source in enumerate(sources):
            copies.append(
                pltpu.make_async_copy(source.at[part], held.at[k, part], sems.at[piece, k])
            )
    for copy in copies:
        copy.start()
    return lambda piece: [c.wait() for c in copies[len(sources) * piece :][: len(sources)]]


def weighed(held, piece):
    depth = PER * FEAT
    return jnp.concatenate(
        [held[k, piece * depth : (piece + 1) * depth, :] for k in range(8)], axis=1
    )


def hidden_kernel(x_ref, own, near, far, *rest):
    *last, out_ref, held, acc, sems = rest
    weights = [pair.at[k] for pair in (own, near, far) for k in range(2)] + last
    wait = fetched(weights, held, sems, PIECES)
    squares, logit = 0.0, 0.0
    for piece in range(PIECES):
        parts = []
        for k in range(PER):
            rows, values, router = gained(x_ref, piece * PER + k)
            squares += jnp.sum(rows * rows, axis=1, keepdims=True)
            logit += jnp.sum(values * router, axis=1, keepdims=True)
            parts.append(values.astype(jnp.bfloat16))
        wait(piece)
        term = jnp.dot(
            jnp.concatenate(parts, axis=1), weighed(held, piece), preferred_element_type=jnp.float32
        )
        acc[...] = term if piece == 0 else acc[...] + term
    rstd = lax.rsqrt(squares / D + EPSILON)
    scale = rstd * jax.nn.sigmoid(logit * rstd)
    for k in range(4):
        gate = acc[:, 256 * k : 256 * k + 128] * scale
        upper = acc[:, 256 * k + 128 : 256 * k + 256] * scale
        out_ref[:, 128 * k : 128 * k + 128] = (jax.nn.silu(gate) * upper).astype(jnp.bfloat16)


def down_kernel(h_ref, d0, d1, d2, d3, out_ref, held, acc, sems):
    wait = fetched((d0, d1, d2, d3), held, sems, DOWN_PIECES)
    each = TENSOR // DOWN_PIECES
    for piece in range(DOWN_PIECES):
        places = range(piece * each, (piece + 1) * each)
        hidden = jnp.concatenate(
            [h for k in places for h in (h_ref[k, :, :256], h_ref[k ^ 1, :, 256:])], axis=1
        )
        wait(piece)
        slices = [held[w, 128 * k : 128 * k + 128, :] for k in places for w in range(4)]
        term = jnp.dot(
            hidden, jnp.concatenate(slices, axis=0), preferred_element_type=jnp.float32
        )
        if piece == 0:
            acc[...] = term
        elif piece < DOWN_PIECES - 1:
            acc[...] += term
        else:
            out_ref[...] = (acc[...] + term).astype(out_ref.dtype)


IN_VMEM = pl.BlockSpec(memory_space=pltpu.VMEM)
IN_HBM = pl.BlockSpec(memory_space=pl.ANY)
PARAMS = pltpu.CompilerParams(vmem_limit_bytes=VMEM)


def left_in_hbm(arrays):
    return [pltpu.with_memory_space_constraint(a, pltpu.HBM) for a in arrays]


def dispatched(ids, tokens, gate, upper):
    return pl.pallas_call(
        dispatch_kernel,
        in_specs=[IN_VMEM, IN_VMEM, IN_HBM, IN_HBM],
        out_specs=[IN_VMEM, IN_HBM],
        out_shape=[
            jax.ShapeDtypeStruct((SLOTS, FEAT), jnp.bfloat16),
            jax.ShapeDtypeStruct((2, D, 128), jnp.bfloat16),
        ],
        scratch_shapes=[
            pltpu.VMEM((2, D, 128), jnp.bfloat16),
            pltpu.SemaphoreType.DMA((2, STAGES, 2)),
        ],
    )(ids, tokens, *left_in_hbm((gate, upper)))


def hidden_units(x, *weights):
    return pl.pallas_call(
        hidden_kernel,
        in_specs=[IN_VMEM] + [IN_HBM] * len(weights),
        out_specs=IN_VMEM,
        out_shape=jax.ShapeDtypeStruct((SLOTS, 512), jnp.bfloat16),
        scratch_shapes=[
            pltpu.VMEM((8, D, 128), jnp.bfloat16),
            pltpu.VMEM((SLOTS, 1024), jnp.float32),
            pltpu.SemaphoreType.DMA((PIECES, 8)),
        ],
        compiler_params=PARAMS,
        cost_estimate=pl.CostEstimate(
            flops=2 * SLOTS * D * 1024,
            bytes_accessed=2 * D * (1024 + SLOTS),
            transcendentals=SLOTS * 512,
        ),
    )(x, *left_in_hbm(weights))


def down_sums(hidden, *weights):
    return pl.pallas_call(
        down_kernel,
        in_specs=[IN_VMEM] + [IN_HBM] * 4,
        out_specs=IN_VMEM,
        out_shape=jax.ShapeDtypeStruct((SLOTS, FEAT), jnp.bfloat16),
        scratch_shapes=[
            pltpu.VMEM((4, 1024, FEAT), jnp.bfloat16),
            pltpu.VMEM((SLOTS, FEAT), jnp.float32),
            pltpu.SemaphoreType.DMA((DOWN_PIECES, 4)),
        ],
        compiler_params=PARAMS,
        cost_estimate=pl.CostEstimate(
            flops=2 * SLOTS * 4096 * FEAT,
            bytes_accessed=2 * 4096 * (FEAT + SLOTS),
            transcendentals=0,
        ),
    )(hidden, *left_in_hbm(weights))


def gathered(array):
    copies = jnp.broadcast_to(array[None], (TENSOR, *array.shape))
    return lax.all_to_all(copies, TENSOR_AXES, 0, 0, tiled=True)


def over_experts(array):
    parts = array.reshape(EXPERTS, CAP, FEAT)
    return lax.all_to_all(parts, "z", 0, 0, tiled=True).reshape(SLOTS, FEAT)


def other_core(array):
    return lax.ppermute(array, "co", [(0, 1), (1, 0)])


def across_border(array):
    return lax.ppermute(array, ("xh", "xl"), [(i, 3 - i) for i in range(4)])


def across_pair(array):
    return lax.ppermute(array, "xl", [(0, 1), (1, 0)])


def tied(*arrays):
    return lax.optimization_barrier(arrays)


def side_rows(norm_gain, router):
    high = norm_gain.astype(jnp.bfloat16)
    rest = norm_gain - high.astype(jnp.float32)
    middle = rest.astype(jnp.bfloat16)
    low = (rest - middle.astype(jnp.float32)).astype(jnp.bfloat16)
    mine = lax.axis_index("z") == jnp.arange(EXPERTS, dtype=jnp.int32)
    column = jnp.sum(jnp.where(mine[None, :], router.astype(jnp.float32), 0.0), axis=1)
    zero = jnp.zeros_like(high)
    return jnp.stack([high, middle, low, column.astype(jnp.bfloat16)] + [zero] * (EXTRA - 4))


def on_device(tokens, norm_gain, router, expert_ids, gate_proj, up_proj, down_proj):
    ids = expert_ids.reshape(1, TOK)
    gate, upper, down = gate_proj[0], up_proj[0], down_proj[0]

    outgoing, own = dispatched(ids, tokens, gate, upper)
    arrived, down_sent, token = tied(over_experts(outgoing), across_pair(down), ids)
    side = side_rows(norm_gain, router)

    near = other_core(own)
    far, down_sent, token = tied(across_border(own), down_sent, token)
    last = [other_core(far[k]) for k in range(2)]

    rows = gathered(jnp.concatenate([arrived, side], axis=0))
    hidden = hidden_units(rows, own, near, far, *last)

    down_far = across_border(down_sent)
    down_near, down_last = other_core(down), other_core(down_far)
    summed = down_sums(gathered(hidden), down, down_near, down_far, down_last)
    returned = over_experts(summed)
    return pl.pallas_call(
        combine_kernel, out_shape=jax.ShapeDtypeStruct((TOK, FEAT), jnp.bfloat16)
    )(token, returned)


def solution(mesh):
    fine = Mesh(
        np.asarray(mesh.devices).reshape(2, 2, 16, 4, 2), ("xh", "co", "z", "y", "xl")
    )
    section, tensor = ("xh", "co"), ("y", "xl")
    in_specs = (
        P((*section, "z"), tensor),
        P(tensor),
        P(tensor, None),
        P((*section, "z"), None),
        P("z", None, (*section, *tensor)),
        P("z", None, (*section, *tensor)),
        P("z", section, tensor),
    )
    return jax.shard_map(
        on_device,
        mesh=fine,
        in_specs=in_specs,
        out_specs=P((*section, "z"), tensor),
        check_vma=False,
    )
```

```python
import jax
import jax.numpy as jnp
import numpy as np
from jax import lax
from jax.experimental import pallas as pl
from jax.experimental.pallas import tpu as pltpu
from jax.sharding import Mesh, PartitionSpec as P

D = 5120
EPSILON = 1e-05
EXPERTS = 16
CAP = 16
SLOTS = EXPERTS * CAP
TOK = 128
FEAT = 640
TENSOR = 8
EXTRA = 8
VMEM = 28 * 1024 * 1024
PIECES = 4
PER = TENSOR // PIECES
DOWN_PIECES = 4
TENSOR_AXES = ("y", "xl")


def column_of(row):
    count = row.shape[1]
    i = lax.broadcasted_iota(jnp.int32, (count, count), 0)
    j = lax.broadcasted_iota(jnp.int32, (count, count), 1)
    return jnp.sum(jnp.where(i == j, row, 0), axis=1, keepdims=True), i, j


def dispatch_kernel(ids_ref, tokens_ref, out_ref):
    row = ids_ref[...]
    col, i, j = column_of(row)
    earlier = jnp.sum(jnp.where((col == row) & (i < j), 1, 0), axis=0, keepdims=True)
    placed = row * CAP + earlier
    slot = lax.broadcasted_iota(jnp.int32, (SLOTS, TOK), 0)
    placing = (slot == placed).astype(jnp.float32).astype(jnp.bfloat16)
    out_ref[...] = jnp.dot(
        placing, tokens_ref[...], preferred_element_type=jnp.float32
    ).astype(jnp.bfloat16)


def combine_kernel(ids_ref, back_ref, out_ref):
    row = ids_ref[...]
    col, i, j = column_of(row)
    earlier = jnp.sum(jnp.where((col == row) & (j < i), 1, 0), axis=1, keepdims=True)
    placed = col * CAP + earlier
    slot = lax.broadcasted_iota(jnp.int32, (TOK, SLOTS), 1)
    placing = (slot == placed).astype(jnp.float32).astype(jnp.bfloat16)
    out_ref[...] = jnp.dot(
        placing, back_ref[...], preferred_element_type=jnp.float32
    ).astype(jnp.bfloat16)


def gained(x_ref, k):
    rows = x_ref[k, :SLOTS, :].astype(jnp.float32)
    more = x_ref[k, SLOTS:, :].astype(jnp.float32)
    return rows, rows * (more[0:1] + more[1:2] + more[2:3]), more[3:4]


def fetched(sources, held, sems, pieces):
    depth = held.shape[1] // pieces
    copies = []
    for piece in range(pieces):
        part = pl.ds(piece * depth, depth)
        for k, source in enumerate(sources):
            copies.append(
                pltpu.make_async_copy(source.at[part], held.at[k, part], sems.at[piece, k])
            )
    for copy in copies:
        copy.start()
    return lambda piece: [c.wait() for c in copies[len(sources) * piece :][: len(sources)]]


def weighed(held, piece):
    depth = PER * FEAT
    return jnp.concatenate(
        [held[k, piece * depth : (piece + 1) * depth, :] for k in range(8)], axis=1
    )


def hidden_kernel(x_ref, *rest):
    *weights, out_ref, held, acc, made, sems, out_sems = rest
    wait = fetched(weights, held, sems, PIECES)
    squares, logit = 0.0, 0.0
    for piece in range(PIECES):
        parts = []
        for k in range(PER):
            rows, values, router = gained(x_ref, piece * PER + k)
            squares += jnp.sum(rows * rows, axis=1, keepdims=True)
            logit += jnp.sum(values * router, axis=1, keepdims=True)
            parts.append(values.astype(jnp.bfloat16))
        wait(piece)
        term = jnp.dot(
            jnp.concatenate(parts, axis=1), weighed(held, piece), preferred_element_type=jnp.float32
        )
        acc[...] = term if piece == 0 else acc[...] + term
    rstd = lax.rsqrt(squares / D + EPSILON)
    scale = rstd * jax.nn.sigmoid(logit * rstd)
    for k in range(4):
        gate = acc[:, 256 * k : 256 * k + 128] * scale
        upper = acc[:, 256 * k + 128 : 256 * k + 256] * scale
        made[:, 128 * k : 128 * k + 128] = (jax.nn.silu(gate) * upper).astype(jnp.bfloat16)
    copies = [
        pltpu.make_async_copy(made, out_ref.at[k], out_sems.at[k]) for k in range(TENSOR)
    ]
    for copy in copies:
        copy.start()
    for copy in copies:
        copy.wait()


def down_kernel(h_ref, d0, d1, d2, d3, out_ref, held, acc, sems):
    wait = fetched((d0, d1, d2, d3), held, sems, DOWN_PIECES)
    each = TENSOR // DOWN_PIECES
    for piece in range(DOWN_PIECES):
        places = range(piece * each, (piece + 1) * each)
        hidden = jnp.concatenate(
            [h for k in places for h in (h_ref[k, :, :256], h_ref[k ^ 1, :, 256:])], axis=1
        )
        wait(piece)
        slices = [held[w, 128 * k : 128 * k + 128, :] for k in places for w in range(4)]
        term = jnp.dot(
            hidden, jnp.concatenate(slices, axis=0), preferred_element_type=jnp.float32
        )
        if piece == 0:
            acc[...] = term
        elif piece < DOWN_PIECES - 1:
            acc[...] += term
        else:
            out_ref[...] = (acc[...] + term).astype(out_ref.dtype)


IN_VMEM = pl.BlockSpec(memory_space=pltpu.VMEM)
IN_HBM = pl.BlockSpec(memory_space=pl.ANY)
PARAMS = pltpu.CompilerParams(vmem_limit_bytes=VMEM)


def left_in_hbm(arrays):
    return [pltpu.with_memory_space_constraint(a, pltpu.HBM) for a in arrays]


def hidden_copies(x, *weights):
    return pl.pallas_call(
        hidden_kernel,
        in_specs=[IN_VMEM] + [IN_HBM] * len(weights),
        out_specs=IN_HBM,
        out_shape=jax.ShapeDtypeStruct((TENSOR, SLOTS, 512), jnp.bfloat16),
        scratch_shapes=[
            pltpu.VMEM((8, D, 128), jnp.bfloat16),
            pltpu.VMEM((SLOTS, 1024), jnp.float32),
            pltpu.VMEM((SLOTS, 512), jnp.bfloat16),
            pltpu.SemaphoreType.DMA((PIECES, 8)),
            pltpu.SemaphoreType.DMA((TENSOR,)),
        ],
        compiler_params=PARAMS,
        cost_estimate=pl.CostEstimate(
            flops=2 * SLOTS * D * 1024,
            bytes_accessed=2 * D * (1024 + SLOTS),
            transcendentals=SLOTS * 512,
        ),
    )(x, *left_in_hbm(weights))


def down_sums(hidden, *weights):
    return pl.pallas_call(
        down_kernel,
        in_specs=[IN_VMEM] + [IN_HBM] * 4,
        out_specs=IN_VMEM,
        out_shape=jax.ShapeDtypeStruct((SLOTS, FEAT), jnp.bfloat16),
        scratch_shapes=[
            pltpu.VMEM((4, 1024, FEAT), jnp.bfloat16),
            pltpu.VMEM((SLOTS, FEAT), jnp.float32),
            pltpu.SemaphoreType.DMA((DOWN_PIECES, 4)),
        ],
        compiler_params=PARAMS,
        cost_estimate=pl.CostEstimate(
            flops=2 * SLOTS * 4096 * FEAT,
            bytes_accessed=2 * 4096 * (FEAT + SLOTS),
            transcendentals=0,
        ),
    )(hidden, *left_in_hbm(weights))


def gathered(copies):
    return lax.all_to_all(copies, TENSOR_AXES, 0, 0, tiled=True)


def over_experts(array):
    parts = array.reshape(EXPERTS, CAP, FEAT)
    return lax.all_to_all(parts, "z", 0, 0, tiled=True).reshape(SLOTS, FEAT)


def other_core(array):
    return lax.ppermute(array, "co", [(0, 1), (1, 0)])


def across_border(array):
    return lax.ppermute(array, ("xh", "xl"), [(i, 3 - i) for i in range(4)])


def across_pair(array):
    return lax.ppermute(array, "xl", [(0, 1), (1, 0)])


def tied(*arrays):
    return lax.optimization_barrier(arrays)


def side_rows(norm_gain, router):
    high = norm_gain.astype(jnp.bfloat16)
    rest = norm_gain - high.astype(jnp.float32)
    middle = rest.astype(jnp.bfloat16)
    low = (rest - middle.astype(jnp.float32)).astype(jnp.bfloat16)
    mine = lax.axis_index("z") == jnp.arange(EXPERTS, dtype=jnp.int32)
    column = jnp.sum(jnp.where(mine[None, :], router.astype(jnp.float32), 0.0), axis=1)
    zero = jnp.zeros_like(high)
    return jnp.stack([high, middle, low, column.astype(jnp.bfloat16)] + [zero] * (EXTRA - 4))


def on_device(tokens, norm_gain, router, expert_ids, gate_proj, up_proj, down_proj):
    ids = expert_ids.reshape(1, TOK)
    gate, upper, down = gate_proj[0], up_proj[0], down_proj[0]

    outgoing = pl.pallas_call(
        dispatch_kernel, out_shape=jax.ShapeDtypeStruct((SLOTS, FEAT), jnp.bfloat16)
    )(ids, tokens)
    pair = (gate, upper)
    arrived, gate_far, down_sent, token = tied(
        over_experts(outgoing), across_border(gate), across_pair(down), ids
    )
    side = side_rows(norm_gain, router)

    near = [other_core(a) for a in pair]
    upper_far, down_sent, token = tied(across_border(upper), down_sent, token)
    far = (gate_far, upper_far)
    last = [other_core(a) for a in far]

    sent = jnp.concatenate([arrived, side], axis=0)
    rows = gathered(jnp.broadcast_to(sent[None], (TENSOR, *sent.shape)))
    hidden = hidden_copies(rows, *pair, *near, *far, *last)

    down_far = across_border(down_sent)
    down_near, down_last = other_core(down), other_core(down_far)
    summed = down_sums(gathered(hidden), down, down_near, down_far, down_last)
    returned = over_experts(summed)
    return pl.pallas_call(
        combine_kernel, out_shape=jax.ShapeDtypeStruct((TOK, FEAT), jnp.bfloat16)
    )(token, returned)


def solution(mesh):
    fine = Mesh(
        np.asarray(mesh.devices).reshape(2, 2, 16, 4, 2), ("xh", "co", "z", "y", "xl")
    )
    section, tensor = ("xh", "co"), ("y", "xl")
    in_specs = (
        P((*section, "z"), tensor),
        P(tensor),
        P(tensor, None),
        P((*section, "z"), None),
        P("z", None, (*section, *tensor)),
        P("z", None, (*section, *tensor)),
        P("z", section, tensor),
    )
    return jax.shard_map(
        on_device,
        mesh=fine,
        in_specs=in_specs,
        out_specs=P((*section, "z"), tensor),
        check_vma=False,
    )
```

```python
import jax
import jax.numpy as jnp
import numpy as np
from jax import lax
from jax.experimental import pallas as pl
from jax.experimental.pallas import tpu as pltpu
from jax.sharding import Mesh, PartitionSpec as P

D = 5120
EPSILON = 1e-05
EXPERTS = 16
CAP = 16
SLOTS = EXPERTS * CAP
TOK = 128
FEAT = 640
TENSOR = 8
EXTRA = 16
VMEM = 28 * 1024 * 1024
PIECES = 4
PER = TENSOR // PIECES
DOWN_PIECES = 4
TENSOR_AXES = ("y", "xl")


def column_of(row):
    count = row.shape[1]
    i = lax.broadcasted_iota(jnp.int32, (count, count), 0)
    j = lax.broadcasted_iota(jnp.int32, (count, count), 1)
    return jnp.sum(jnp.where(i == j, row, 0), axis=1, keepdims=True), i, j


def dispatch_kernel(ids_ref, tokens_ref, out_ref):
    row = ids_ref[...]
    col, i, j = column_of(row)
    earlier = jnp.sum(jnp.where((col == row) & (i < j), 1, 0), axis=0, keepdims=True)
    placed = row * CAP + earlier
    slot = lax.broadcasted_iota(jnp.int32, (SLOTS, TOK), 0)
    placing = (slot == placed).astype(jnp.float32).astype(jnp.bfloat16)
    out_ref[...] = jnp.dot(
        placing, tokens_ref[...], preferred_element_type=jnp.float32
    ).astype(jnp.bfloat16)


def combine_kernel(ids_ref, back_ref, out_ref):
    row = ids_ref[...]
    col, i, j = column_of(row)
    earlier = jnp.sum(jnp.where((col == row) & (j < i), 1, 0), axis=1, keepdims=True)
    placed = col * CAP + earlier
    slot = lax.broadcasted_iota(jnp.int32, (TOK, SLOTS), 1)
    placing = (slot == placed).astype(jnp.float32).astype(jnp.bfloat16)
    out_ref[...] = jnp.dot(
        placing, back_ref[...], preferred_element_type=jnp.float32
    ).astype(jnp.bfloat16)


def gained(x_ref, k):
    rows = x_ref[k, :SLOTS, :].astype(jnp.float32)
    more = x_ref[k, SLOTS:, :].astype(jnp.float32)
    return rows, rows * (more[0:1] + more[1:2] + more[2:3]), more[3:4]


def fetched(sources, held, sems, pieces):
    depth = held.shape[1] // pieces
    copies = []
    for piece in range(pieces):
        part = pl.ds(piece * depth, depth)
        for k, source in enumerate(sources):
            copies.append(
                pltpu.make_async_copy(source.at[part], held.at[k, part], sems.at[piece, k])
            )
    for copy in copies:
        copy.start()
    return lambda piece: [c.wait() for c in copies[len(sources) * piece :][: len(sources)]]


def weighed(held, piece):
    depth = PER * FEAT
    return jnp.concatenate(
        [held[k, piece * depth : (piece + 1) * depth, :] for k in range(8)], axis=1
    )


def hidden_kernel(x_ref, *rest):
    *weights, out_ref, held, acc, made, sems, out_sems = rest
    wait = fetched(weights, held, sems, PIECES)
    squares, logit = 0.0, 0.0
    for piece in range(PIECES):
        parts = []
        for k in range(PER):
            rows, values, router = gained(x_ref, piece * PER + k)
            squares += jnp.sum(rows * rows, axis=1, keepdims=True)
            logit += jnp.sum(values * router, axis=1, keepdims=True)
            parts.append(values.astype(jnp.bfloat16))
        wait(piece)
        term = jnp.dot(
            jnp.concatenate(parts, axis=1), weighed(held, piece), preferred_element_type=jnp.float32
        )
        acc[...] = term if piece == 0 else acc[...] + term
    rstd = lax.rsqrt(squares / D + EPSILON)
    scale = rstd * jax.nn.sigmoid(logit * rstd)
    for k in range(4):
        gate = acc[:, 256 * k : 256 * k + 128] * scale
        upper = acc[:, 256 * k + 128 : 256 * k + 256] * scale
        made[:, 128 * k : 128 * k + 128] = (jax.nn.silu(gate) * upper).astype(jnp.bfloat16)
    copies = [
        pltpu.make_async_copy(made, out_ref.at[k], out_sems.at[k]) for k in range(TENSOR)
    ]
    for copy in copies:
        copy.start()
    for copy in copies:
        copy.wait()


def down_kernel(h_ref, d0, d1, d2, d3, out_ref, held, acc, sems):
    wait = fetched((d0, d1, d2, d3), held, sems, DOWN_PIECES)
    each = TENSOR // DOWN_PIECES
    for piece in range(DOWN_PIECES):
        places = range(piece * each, (piece + 1) * each)
        hidden = jnp.concatenate(
            [h for k in places for h in (h_ref[k, :, :256], h_ref[k ^ 1, :, 256:])], axis=1
        )
        wait(piece)
        slices = [held[w, 128 * k : 128 * k + 128, :] for k in places for w in range(4)]
        term = jnp.dot(
            hidden, jnp.concatenate(slices, axis=0), preferred_element_type=jnp.float32
        )
        if piece == 0:
            acc[...] = term
        elif piece < DOWN_PIECES - 1:
            acc[...] += term
        else:
            out_ref[...] = (acc[...] + term).astype(out_ref.dtype)


IN_VMEM = pl.BlockSpec(memory_space=pltpu.VMEM)
IN_HBM = pl.BlockSpec(memory_space=pl.ANY)
PARAMS = pltpu.CompilerParams(vmem_limit_bytes=VMEM)
SMALL = pltpu.CompilerParams(vmem_limit_bytes=8 * 1024 * 1024)


def left_in_hbm(arrays):
    return [pltpu.with_memory_space_constraint(a, pltpu.HBM) for a in arrays]


def hidden_copies(x, *weights):
    return pl.pallas_call(
        hidden_kernel,
        in_specs=[IN_VMEM] + [IN_HBM] * len(weights),
        out_specs=IN_HBM,
        out_shape=pltpu.HBM((TENSOR, SLOTS, 512), jnp.bfloat16),
        scratch_shapes=[
            pltpu.VMEM((8, D, 128), jnp.bfloat16),
            pltpu.VMEM((SLOTS, 1024), jnp.float32),
            pltpu.VMEM((SLOTS, 512), jnp.bfloat16),
            pltpu.SemaphoreType.DMA((PIECES, 8)),
            pltpu.SemaphoreType.DMA((TENSOR,)),
        ],
        compiler_params=PARAMS,
        cost_estimate=pl.CostEstimate(
            flops=2 * SLOTS * D * 1024,
            bytes_accessed=2 * D * (1024 + SLOTS),
            transcendentals=SLOTS * 512,
        ),
    )(x, *left_in_hbm(weights))


def spread_kernel(rows_ref, side_ref, out_ref, sems):
    copies = []
    for k in range(TENSOR):
        for n, (ref, part) in enumerate(
            ((rows_ref, pl.ds(0, SLOTS)), (side_ref, pl.ds(SLOTS, EXTRA)))
        ):
            copies.append(pltpu.make_async_copy(ref, out_ref.at[k, part], sems.at[n, k]))
    for copy in copies:
        copy.start()
    for copy in copies:
        copy.wait()


def row_copies(rows, side):
    return pl.pallas_call(
        spread_kernel,
        in_specs=[IN_VMEM, IN_VMEM],
        out_specs=IN_HBM,
        out_shape=pltpu.HBM((TENSOR, SLOTS + EXTRA, FEAT), jnp.bfloat16),
        scratch_shapes=[pltpu.SemaphoreType.DMA((2, TENSOR))],
        compiler_params=SMALL,
    )(rows, side)


def down_sums(hidden, *weights):
    return pl.pallas_call(
        down_kernel,
        in_specs=[IN_VMEM] + [IN_HBM] * 4,
        out_specs=IN_VMEM,
        out_shape=jax.ShapeDtypeStruct((SLOTS, FEAT), jnp.bfloat16),
        scratch_shapes=[
            pltpu.VMEM((4, 1024, FEAT), jnp.bfloat16),
            pltpu.VMEM((SLOTS, FEAT), jnp.float32),
            pltpu.SemaphoreType.DMA((DOWN_PIECES, 4)),
        ],
        compiler_params=PARAMS,
        cost_estimate=pl.CostEstimate(
            flops=2 * SLOTS * 4096 * FEAT,
            bytes_accessed=2 * 4096 * (FEAT + SLOTS),
            transcendentals=0,
        ),
    )(hidden, *left_in_hbm(weights))


def gathered(copies):
    return lax.all_to_all(copies, TENSOR_AXES, 0, 0, tiled=True)


def over_experts(array):
    parts = array.reshape(EXPERTS, CAP, FEAT)
    return lax.all_to_all(parts, "z", 0, 0, tiled=True).reshape(SLOTS, FEAT)


def other_core(array):
    return lax.ppermute(array, "co", [(0, 1), (1, 0)])


def across_border(array):
    return lax.ppermute(array, ("xh", "xl"), [(i, 3 - i) for i in range(4)])


def across_pair(array):
    return lax.ppermute(array, "xl", [(0, 1), (1, 0)])


def tied(*arrays):
    return lax.optimization_barrier(arrays)


def side_rows(norm_gain, router):
    high = norm_gain.astype(jnp.bfloat16)
    rest = norm_gain - high.astype(jnp.float32)
    middle = rest.astype(jnp.bfloat16)
    low = (rest - middle.astype(jnp.float32)).astype(jnp.bfloat16)
    mine = lax.axis_index("z") == jnp.arange(EXPERTS, dtype=jnp.int32)
    column = jnp.sum(jnp.where(mine[None, :], router.astype(jnp.float32), 0.0), axis=1)
    zero = jnp.zeros_like(high)
    return jnp.stack([high, middle, low, column.astype(jnp.bfloat16)] + [zero] * (EXTRA - 4))


def on_device(tokens, norm_gain, router, expert_ids, gate_proj, up_proj, down_proj):
    ids = expert_ids.reshape(1, TOK)
    gate, upper, down = gate_proj[0], up_proj[0], down_proj[0]

    outgoing = pl.pallas_call(
        dispatch_kernel, out_shape=jax.ShapeDtypeStruct((SLOTS, FEAT), jnp.bfloat16)
    )(ids, tokens)
    pair = (gate, upper)
    arrived, gate_far, down_sent, token = tied(
        over_experts(outgoing), across_border(gate), across_pair(down), ids
    )
    side = side_rows(norm_gain, router)

    near = [other_core(a) for a in pair]
    upper_far, down_sent, token = tied(across_border(upper), down_sent, token)
    far = (gate_far, upper_far)
    last = [other_core(a) for a in far]

    rows = gathered(row_copies(arrived, side))
    hidden = hidden_copies(rows, *pair, *near, *far, *last)

    down_far = across_border(down_sent)
    down_near, down_last = other_core(down), other_core(down_far)
    summed = down_sums(gathered(hidden), down, down_near, down_far, down_last)
    returned = over_experts(summed)
    return pl.pallas_call(
        combine_kernel,
        out_shape=jax.ShapeDtypeStruct((TOK, FEAT), jnp.bfloat16),
        compiler_params=SMALL,
    )(token, returned)


def solution(mesh):
    fine = Mesh(
        np.asarray(mesh.devices).reshape(2, 2, 16, 4, 2), ("xh", "co", "z", "y", "xl")
    )
    section, tensor = ("xh", "co"), ("y", "xl")
    in_specs = (
        P((*section, "z"), tensor),
        P(tensor),
        P(tensor, None),
        P((*section, "z"), None),
        P("z", None, (*section, *tensor)),
        P("z", None, (*section, *tensor)),
        P("z", section, tensor),
    )
    return jax.shard_map(
        on_device,
        mesh=fine,
        in_specs=in_specs,
        out_specs=P((*section, "z"), tensor),
        check_vma=False,
    )
```

```python
import jax
import jax.numpy as jnp
import numpy as np
from jax import lax
from jax.experimental import pallas as pl
from jax.experimental.pallas import tpu as pltpu
from jax.sharding import Mesh, PartitionSpec as P

D = 5120
EPSILON = 1e-05
EXPERTS = 16
CAP = 16
SLOTS = EXPERTS * CAP
TOK = 128
FEAT = 640
TENSOR = 8
EXTRA = 16
VMEM = 28 * 1024 * 1024
PIECES = 2
PER = TENSOR // PIECES
DOWN_PIECES = 2
TENSOR_AXES = ("y", "xl")


def column_of(row):
    count = row.shape[1]
    i = lax.broadcasted_iota(jnp.int32, (count, count), 0)
    j = lax.broadcasted_iota(jnp.int32, (count, count), 1)
    return jnp.sum(jnp.where(i == j, row, 0), axis=1, keepdims=True), i, j


def dispatch_kernel(ids_ref, tokens_ref, out_ref, held, made, sems):
    inward = pltpu.make_async_copy(tokens_ref, held, sems.at[0])
    inward.start()
    row = ids_ref[...]
    col, i, j = column_of(row)
    earlier = jnp.sum(jnp.where((col == row) & (i < j), 1, 0), axis=0, keepdims=True)
    placed = row * CAP + earlier
    slot = lax.broadcasted_iota(jnp.int32, (SLOTS, TOK), 0)
    placing = (slot == placed).astype(jnp.float32).astype(jnp.bfloat16)
    inward.wait()
    half, outward = SLOTS // 2, []
    for k in range(2):
        made[k] = jnp.dot(
            placing[half * k : half * k + half], held[...], preferred_element_type=jnp.float32
        ).astype(jnp.bfloat16)
        outward.append(
            pltpu.make_async_copy(
                made.at[k], out_ref.at[pl.ds(half * k, half)], sems.at[1 + k]
            )
        )
        outward[k].start()
    for copy in outward:
        copy.wait()


def combine_kernel(ids_ref, back_ref, out_ref):
    row = ids_ref[...]
    col, i, j = column_of(row)
    earlier = jnp.sum(jnp.where((col == row) & (j < i), 1, 0), axis=1, keepdims=True)
    placed = col * CAP + earlier
    slot = lax.broadcasted_iota(jnp.int32, (TOK, SLOTS), 1)
    placing = (slot == placed).astype(jnp.float32).astype(jnp.bfloat16)
    out_ref[...] = jnp.dot(
        placing, back_ref[...], preferred_element_type=jnp.float32
    ).astype(jnp.bfloat16)


def gained(x_ref, k):
    rows = x_ref[k, :SLOTS, :].astype(jnp.float32)
    more = x_ref[k, SLOTS:, :].astype(jnp.float32)
    return rows, rows * (more[0:1] + more[1:2] + more[2:3]), more[3:4]


def fetched(sources, held, sems, pieces):
    depth = held.shape[1] // pieces
    copies = []
    for piece in range(pieces):
        part = pl.ds(piece * depth, depth)
        for k, source in enumerate(sources):
            copies.append(
                pltpu.make_async_copy(source.at[part], held.at[k, part], sems.at[piece, k])
            )
    for copy in copies:
        copy.start()
    return lambda piece: [c.wait() for c in copies[len(sources) * piece :][: len(sources)]]


def weighed(held, piece):
    depth = PER * FEAT
    return jnp.concatenate(
        [held[k, piece * depth : (piece + 1) * depth, :] for k in range(8)], axis=1
    )


def hidden_kernel(x_ref, *rest):
    *weights, out_ref, held, acc, made, sems, out_sems = rest
    wait = fetched(weights, held, sems, PIECES)
    squares, logit = 0.0, 0.0
    for piece in range(PIECES):
        parts = []
        for k in range(PER):
            rows, values, router = gained(x_ref, piece * PER + k)
            squares += jnp.sum(rows * rows, axis=1, keepdims=True)
            logit += jnp.sum(values * router, axis=1, keepdims=True)
            parts.append(values.astype(jnp.bfloat16))
        wait(piece)
        term = jnp.dot(
            jnp.concatenate(parts, axis=1), weighed(held, piece), preferred_element_type=jnp.float32
        )
        acc[...] = term if piece == 0 else acc[...] + term
    rstd = lax.rsqrt(squares / D + EPSILON)
    scale = rstd * jax.nn.sigmoid(logit * rstd)
    for k in range(4):
        gate = acc[:, 256 * k : 256 * k + 128] * scale
        upper = acc[:, 256 * k + 128 : 256 * k + 256] * scale
        made[:, 128 * k : 128 * k + 128] = (jax.nn.silu(gate) * upper).astype(jnp.bfloat16)
    copies = [
        pltpu.make_async_copy(made, out_ref.at[k], out_sems.at[k]) for k in range(TENSOR)
    ]
    for copy in copies:
        copy.start()
    for copy in copies:
        copy.wait()


def down_kernel(h_ref, d0, d1, d2, d3, out_ref, held, acc, sems):
    wait = fetched((d0, d1, d2, d3), held, sems, DOWN_PIECES)
    each = TENSOR // DOWN_PIECES
    for piece in range(DOWN_PIECES):
        places = range(piece * each, (piece + 1) * each)
        hidden = jnp.concatenate(
            [h for k in places for h in (h_ref[k, :, :256], h_ref[k ^ 1, :, 256:])], axis=1
        )
        wait(piece)
        slices = [held[w, 128 * k : 128 * k + 128, :] for k in places for w in range(4)]
        term = jnp.dot(
            hidden, jnp.concatenate(slices, axis=0), preferred_element_type=jnp.float32
        )
        if piece == 0:
            acc[...] = term
        elif piece < DOWN_PIECES - 1:
            acc[...] += term
        else:
            out_ref[...] = (acc[...] + term).astype(out_ref.dtype)


IN_VMEM = pl.BlockSpec(memory_space=pltpu.VMEM)
IN_HBM = pl.BlockSpec(memory_space=pl.ANY)
PARAMS = pltpu.CompilerParams(vmem_limit_bytes=VMEM)
SMALL = pltpu.CompilerParams(vmem_limit_bytes=8 * 1024 * 1024)


def left_in_hbm(arrays):
    return [pltpu.with_memory_space_constraint(a, pltpu.HBM) for a in arrays]


def hidden_copies(x, *weights):
    return pl.pallas_call(
        hidden_kernel,
        in_specs=[IN_VMEM] + [IN_HBM] * len(weights),
        out_specs=IN_HBM,
        out_shape=pltpu.HBM((TENSOR, SLOTS, 512), jnp.bfloat16),
        scratch_shapes=[
            pltpu.VMEM((8, D, 128), jnp.bfloat16),
            pltpu.VMEM((SLOTS, 1024), jnp.float32),
            pltpu.VMEM((SLOTS, 512), jnp.bfloat16),
            pltpu.SemaphoreType.DMA((PIECES, 8)),
            pltpu.SemaphoreType.DMA((TENSOR,)),
        ],
        compiler_params=PARAMS,
        cost_estimate=pl.CostEstimate(
            flops=2 * SLOTS * D * 1024,
            bytes_accessed=2 * D * (1024 + SLOTS),
            transcendentals=SLOTS * 512,
        ),
    )(x, *left_in_hbm(weights))


def spread_kernel(rows_ref, side_ref, out_ref, sems):
    copies = []
    for k in range(TENSOR):
        for n, (ref, part) in enumerate(
            ((rows_ref, pl.ds(0, SLOTS)), (side_ref, pl.ds(SLOTS, EXTRA)))
        ):
            copies.append(pltpu.make_async_copy(ref, out_ref.at[k, part], sems.at[n, k]))
    for copy in copies:
        copy.start()
    for copy in copies:
        copy.wait()


def row_copies(rows, side):
    return pl.pallas_call(
        spread_kernel,
        in_specs=[IN_VMEM, IN_VMEM],
        out_specs=IN_HBM,
        out_shape=pltpu.HBM((TENSOR, SLOTS + EXTRA, FEAT), jnp.bfloat16),
        scratch_shapes=[pltpu.SemaphoreType.DMA((2, TENSOR))],
        compiler_params=SMALL,
    )(rows, side)


def down_sums(hidden, *weights):
    return pl.pallas_call(
        down_kernel,
        in_specs=[IN_VMEM] + [IN_HBM] * 4,
        out_specs=IN_VMEM,
        out_shape=jax.ShapeDtypeStruct((SLOTS, FEAT), jnp.bfloat16),
        scratch_shapes=[
            pltpu.VMEM((4, 1024, FEAT), jnp.bfloat16),
            pltpu.VMEM((SLOTS, FEAT), jnp.float32),
            pltpu.SemaphoreType.DMA((DOWN_PIECES, 4)),
        ],
        compiler_params=PARAMS,
        cost_estimate=pl.CostEstimate(
            flops=2 * SLOTS * 4096 * FEAT,
            bytes_accessed=2 * 4096 * (FEAT + SLOTS),
            transcendentals=0,
        ),
    )(hidden, *left_in_hbm(weights))


def gathered(copies):
    return lax.all_to_all(copies, TENSOR_AXES, 0, 0, tiled=True)


def over_experts(array):
    parts = array.reshape(EXPERTS, CAP, FEAT)
    return lax.all_to_all(parts, "z", 0, 0, tiled=True).reshape(SLOTS, FEAT)


def other_core(array):
    return lax.ppermute(array, "co", [(0, 1), (1, 0)])


def across_border(array):
    return lax.ppermute(array, ("xh", "xl"), [(i, 3 - i) for i in range(4)])


def across_pair(array):
    return lax.ppermute(array, "xl", [(0, 1), (1, 0)])


def tied(*arrays):
    return lax.optimization_barrier(arrays)


def side_rows(norm_gain, router):
    high = norm_gain.astype(jnp.bfloat16)
    rest = norm_gain - high.astype(jnp.float32)
    middle = rest.astype(jnp.bfloat16)
    low = (rest - middle.astype(jnp.float32)).astype(jnp.bfloat16)
    mine = lax.axis_index("z") == jnp.arange(EXPERTS, dtype=jnp.int32)
    column = jnp.sum(jnp.where(mine[None, :], router.astype(jnp.float32), 0.0), axis=1)
    zero = jnp.zeros_like(high)
    return jnp.stack([high, middle, low, column.astype(jnp.bfloat16)] + [zero] * (EXTRA - 4))


def on_device(tokens, norm_gain, router, expert_ids, gate_proj, up_proj, down_proj):
    ids = expert_ids.reshape(1, TOK)
    gate, upper, down = gate_proj[0], up_proj[0], down_proj[0]

    outgoing = pl.pallas_call(
        dispatch_kernel,
        in_specs=[IN_VMEM, IN_HBM],
        out_specs=IN_HBM,
        out_shape=pltpu.HBM((SLOTS, FEAT), jnp.bfloat16),
        scratch_shapes=[
            pltpu.VMEM((TOK, FEAT), jnp.bfloat16),
            pltpu.VMEM((2, SLOTS // 2, FEAT), jnp.bfloat16),
            pltpu.SemaphoreType.DMA((3,)),
        ],
    )(ids, *left_in_hbm((tokens,)))
    pair = (gate, upper)
    arrived, gate_far, down_sent, token = tied(
        over_experts(outgoing), across_border(gate), across_pair(down), ids
    )
    side = side_rows(norm_gain, router)

    near = [other_core(a) for a in pair]
    upper_far, down_sent, token = tied(across_border(upper), down_sent, token)
    far = (gate_far, upper_far)
    last = [other_core(a) for a in far]

    rows = gathered(row_copies(arrived, side))
    hidden = hidden_copies(rows, *pair, *near, *far, *last)

    down_far = across_border(down_sent)
    down_near, down_last = other_core(down), other_core(down_far)
    summed = down_sums(gathered(hidden), down, down_near, down_far, down_last)
    returned = over_experts(summed)
    return pl.pallas_call(
        combine_kernel,
        out_shape=jax.ShapeDtypeStruct((TOK, FEAT), jnp.bfloat16),
        compiler_params=SMALL,
    )(token, returned)


def solution(mesh):
    fine = Mesh(
        np.asarray(mesh.devices).reshape(2, 2, 16, 4, 2), ("xh", "co", "z", "y", "xl")
    )
    section, tensor = ("xh", "co"), ("y", "xl")
    in_specs = (
        P((*section, "z"), tensor),
        P(tensor),
        P(tensor, None),
        P((*section, "z"), None),
        P("z", None, (*section, *tensor)),
        P("z", None, (*section, *tensor)),
        P("z", section, tensor),
    )
    return jax.shard_map(
        on_device,
        mesh=fine,
        in_specs=in_specs,
        out_specs=P((*section, "z"), tensor),
        check_vma=False,
    )
```

```python
import jax
import jax.numpy as jnp
import numpy as np
from jax import lax
from jax.experimental import pallas as pl
from jax.experimental.pallas import tpu as pltpu
from jax.sharding import Mesh, PartitionSpec as P

D = 5120
EPSILON = 1e-05
EXPERTS = 16
CAP = 16
SLOTS = EXPERTS * CAP
TOK = 128
FEAT = 640
TENSOR = 8
EXTRA = 16
VMEM = 28 * 1024 * 1024
PIECES = 4
PER = TENSOR // PIECES
DOWN_PIECES = 4
TENSOR_AXES = ("y", "xl")


def column_of(row):
    count = row.shape[1]
    i = lax.broadcasted_iota(jnp.int32, (count, count), 0)
    j = lax.broadcasted_iota(jnp.int32, (count, count), 1)
    return jnp.sum(jnp.where(i == j, row, 0), axis=1, keepdims=True), i, j


def dispatch_kernel(ids_ref, tokens_ref, out_ref):
    row = ids_ref[...]
    col, i, j = column_of(row)
    earlier = jnp.sum(jnp.where((col == row) & (i < j), 1, 0), axis=0, keepdims=True)
    placed = row * CAP + earlier
    slot = lax.broadcasted_iota(jnp.int32, (SLOTS, TOK), 0)
    placing = (slot == placed).astype(jnp.float32).astype(jnp.bfloat16)
    out_ref[...] = jnp.dot(
        placing, tokens_ref[...], preferred_element_type=jnp.float32
    ).astype(jnp.bfloat16)


def combine_kernel(ids_ref, back_ref, out_ref):
    row = ids_ref[...]
    col, i, j = column_of(row)
    earlier = jnp.sum(jnp.where((col == row) & (j < i), 1, 0), axis=1, keepdims=True)
    placed = col * CAP + earlier
    slot = lax.broadcasted_iota(jnp.int32, (TOK, SLOTS), 1)
    placing = (slot == placed).astype(jnp.float32).astype(jnp.bfloat16)
    out_ref[...] = jnp.dot(
        placing, back_ref[...], preferred_element_type=jnp.float32
    ).astype(jnp.bfloat16)


def gained(x_ref, k):
    rows = x_ref[k, :SLOTS, :].astype(jnp.float32)
    more = x_ref[k, SLOTS:, :].astype(jnp.float32)
    return rows, rows * (more[0:1] + more[1:2] + more[2:3]), more[3:4]


def fetched(sources, held, sems, pieces):
    depth = held.shape[1] // pieces
    copies = []
    for piece in range(pieces):
        part = pl.ds(piece * depth, depth)
        for k, source in enumerate(sources):
            copies.append(
                pltpu.make_async_copy(source.at[part], held.at[k, part], sems.at[piece, k])
            )
    for copy in copies:
        copy.start()
    return lambda piece: [c.wait() for c in copies[len(sources) * piece :][: len(sources)]]


def weighed(held, piece, places):
    depth = PER * FEAT
    return jnp.concatenate(
        [held[k, piece * depth : (piece + 1) * depth, :] for k in places], axis=1
    )


def hidden_kernel(x_ref, *rest):
    *weights, out_ref, held, acc, made, sems, out_sems = rest
    wait = fetched(weights, held, sems, PIECES)
    squares, logit = 0.0, 0.0
    for piece in range(PIECES):
        parts = []
        for k in range(PER):
            rows, values, router = gained(x_ref, piece * PER + k)
            squares += jnp.sum(rows * rows, axis=1, keepdims=True)
            logit += jnp.sum(values * router, axis=1, keepdims=True)
            parts.append(values.astype(jnp.bfloat16))
        values = jnp.concatenate(parts, axis=1)
        wait(piece)
        if piece < PIECES - 1:
            term = jnp.dot(
                values, weighed(held, piece, range(8)), preferred_element_type=jnp.float32
            )
            acc[...] = term if piece == 0 else acc[...] + term
    rstd = lax.rsqrt(squares / D + EPSILON)
    scale = rstd * jax.nn.sigmoid(logit * rstd)
    copies = []
    for q in range(4):
        term = acc[:, 256 * q : 256 * q + 256] + jnp.dot(
            values,
            weighed(held, PIECES - 1, (2 * q, 2 * q + 1)),
            preferred_element_type=jnp.float32,
        )
        gate, upper = term[:, :128] * scale, term[:, 128:] * scale
        made[q] = (jax.nn.silu(gate) * upper).astype(jnp.bfloat16)
        for k in range(TENSOR):
            copy = pltpu.make_async_copy(
                made.at[q], out_ref.at[k, :, pl.ds(128 * q, 128)], out_sems.at[q, k]
            )
            copy.start()
            copies.append(copy)
    for copy in copies:
        copy.wait()


def down_kernel(h_ref, d0, d1, d2, d3, out_ref, held, acc, sems):
    wait = fetched((d0, d1, d2, d3), held, sems, DOWN_PIECES)
    each = TENSOR // DOWN_PIECES
    for piece in range(DOWN_PIECES):
        places = range(piece * each, (piece + 1) * each)
        hidden = jnp.concatenate(
            [h for k in places for h in (h_ref[k, :, :256], h_ref[k ^ 1, :, 256:])], axis=1
        )
        wait(piece)
        slices = [held[w, 128 * k : 128 * k + 128, :] for k in places for w in range(4)]
        term = jnp.dot(
            hidden, jnp.concatenate(slices, axis=0), preferred_element_type=jnp.float32
        )
        if piece == 0:
            acc[...] = term
        elif piece < DOWN_PIECES - 1:
            acc[...] += term
        else:
            out_ref[...] = (acc[...] + term).astype(out_ref.dtype)


IN_VMEM = pl.BlockSpec(memory_space=pltpu.VMEM)
IN_HBM = pl.BlockSpec(memory_space=pl.ANY)
PARAMS = pltpu.CompilerParams(vmem_limit_bytes=VMEM)
SMALL = pltpu.CompilerParams(vmem_limit_bytes=8 * 1024 * 1024)


def left_in_hbm(arrays):
    return [pltpu.with_memory_space_constraint(a, pltpu.HBM) for a in arrays]


def hidden_copies(x, *weights):
    return pl.pallas_call(
        hidden_kernel,
        in_specs=[IN_VMEM] + [IN_HBM] * len(weights),
        out_specs=IN_HBM,
        out_shape=pltpu.HBM((TENSOR, SLOTS, 512), jnp.bfloat16),
        scratch_shapes=[
            pltpu.VMEM((8, D, 128), jnp.bfloat16),
            pltpu.VMEM((SLOTS, 1024), jnp.float32),
            pltpu.VMEM((4, SLOTS, 128), jnp.bfloat16),
            pltpu.SemaphoreType.DMA((PIECES, 8)),
            pltpu.SemaphoreType.DMA((4, TENSOR)),
        ],
        compiler_params=PARAMS,
        cost_estimate=pl.CostEstimate(
            flops=2 * SLOTS * D * 1024,
            bytes_accessed=2 * D * (1024 + SLOTS),
            transcendentals=SLOTS * 512,
        ),
    )(x, *left_in_hbm(weights))


def spread_kernel(rows_ref, side_ref, out_ref, sems):
    copies = []
    for k in range(TENSOR):
        for n, (ref, part) in enumerate(
            ((rows_ref, pl.ds(0, SLOTS)), (side_ref, pl.ds(SLOTS, EXTRA)))
        ):
            copies.append(pltpu.make_async_copy(ref, out_ref.at[k, part], sems.at[n, k]))
    for copy in copies:
        copy.start()
    for copy in copies:
        copy.wait()


def row_copies(rows, side):
    return pl.pallas_call(
        spread_kernel,
        in_specs=[IN_VMEM, IN_VMEM],
        out_specs=IN_HBM,
        out_shape=pltpu.HBM((TENSOR, SLOTS + EXTRA, FEAT), jnp.bfloat16),
        scratch_shapes=[pltpu.SemaphoreType.DMA((2, TENSOR))],
        compiler_params=SMALL,
    )(rows, side)


def down_sums(hidden, *weights):
    return pl.pallas_call(
        down_kernel,
        in_specs=[IN_VMEM] + [IN_HBM] * 4,
        out_specs=IN_VMEM,
        out_shape=jax.ShapeDtypeStruct((SLOTS, FEAT), jnp.bfloat16),
        scratch_shapes=[
            pltpu.VMEM((4, 1024, FEAT), jnp.bfloat16),
            pltpu.VMEM((SLOTS, FEAT), jnp.float32),
            pltpu.SemaphoreType.DMA((DOWN_PIECES, 4)),
        ],
        compiler_params=PARAMS,
        cost_estimate=pl.CostEstimate(
            flops=2 * SLOTS * 4096 * FEAT,
            bytes_accessed=2 * 4096 * (FEAT + SLOTS),
            transcendentals=0,
        ),
    )(hidden, *left_in_hbm(weights))


def gathered(copies):
    return lax.all_to_all(copies, TENSOR_AXES, 0, 0, tiled=True)


def over_experts(array):
    parts = array.reshape(EXPERTS, CAP, FEAT)
    return lax.all_to_all(parts, "z", 0, 0, tiled=True).reshape(SLOTS, FEAT)


def other_core(array):
    return lax.ppermute(array, "co", [(0, 1), (1, 0)])


def across_border(array):
    return lax.ppermute(array, ("xh", "xl"), [(i, 3 - i) for i in range(4)])


def across_pair(array):
    return lax.ppermute(array, "xl", [(0, 1), (1, 0)])


def tied(*arrays):
    return lax.optimization_barrier(arrays)


def side_rows(norm_gain, router):
    high = norm_gain.astype(jnp.bfloat16)
    rest = norm_gain - high.astype(jnp.float32)
    middle = rest.astype(jnp.bfloat16)
    low = (rest - middle.astype(jnp.float32)).astype(jnp.bfloat16)
    mine = lax.axis_index("z") == jnp.arange(EXPERTS, dtype=jnp.int32)
    column = jnp.sum(jnp.where(mine[None, :], router.astype(jnp.float32), 0.0), axis=1)
    zero = jnp.zeros_like(high)
    return jnp.stack([high, middle, low, column.astype(jnp.bfloat16)] + [zero] * (EXTRA - 4))


def on_device(tokens, norm_gain, router, expert_ids, gate_proj, up_proj, down_proj):
    ids = expert_ids.reshape(1, TOK)
    gate, upper, down = gate_proj[0], up_proj[0], down_proj[0]

    outgoing = pl.pallas_call(
        dispatch_kernel, out_shape=jax.ShapeDtypeStruct((SLOTS, FEAT), jnp.bfloat16)
    )(ids, tokens)
    pair = (gate, upper)
    arrived, gate_far, down_sent, token = tied(
        over_experts(outgoing), across_border(gate), across_pair(down), ids
    )
    side = side_rows(norm_gain, router)

    near = [other_core(a) for a in pair]
    upper_far, down_sent, token = tied(across_border(upper), down_sent, token)
    far = (gate_far, upper_far)
    last = [other_core(a) for a in far]

    rows = gathered(row_copies(arrived, side))
    hidden = hidden_copies(rows, *pair, *near, *far, *last)

    down_far = across_border(down_sent)
    down_near, down_last = other_core(down), other_core(down_far)
    summed = down_sums(gathered(hidden), down, down_near, down_far, down_last)
    returned = over_experts(summed)
    return pl.pallas_call(
        combine_kernel,
        out_shape=jax.ShapeDtypeStruct((TOK, FEAT), jnp.bfloat16),
        compiler_params=SMALL,
    )(token, returned)


def solution(mesh):
    fine = Mesh(
        np.asarray(mesh.devices).reshape(2, 2, 16, 4, 2), ("xh", "co", "z", "y", "xl")
    )
    section, tensor = ("xh", "co"), ("y", "xl")
    in_specs = (
        P((*section, "z"), tensor),
        P(tensor),
        P(tensor, None),
        P((*section, "z"), None),
        P("z", None, (*section, *tensor)),
        P("z", None, (*section, *tensor)),
        P("z", section, tensor),
    )
    return jax.shard_map(
        on_device,
        mesh=fine,
        in_specs=in_specs,
        out_specs=P((*section, "z"), tensor),
        check_vma=False,
    )
```

```python
import jax
import jax.numpy as jnp
import numpy as np
from jax import lax
from jax.experimental import pallas as pl
from jax.experimental.pallas import tpu as pltpu
from jax.sharding import Mesh, PartitionSpec as P

D = 5120
EPSILON = 1e-05
EXPERTS = 16
CAP = 16
SLOTS = EXPERTS * CAP
TOK = 128
FEAT = 640
TENSOR = 8
EXTRA = 16
VMEM = 28 * 1024 * 1024
PIECES = 4
PER = TENSOR // PIECES
DOWN_PIECES = 4
TENSOR_AXES = ("y", "xl")


def column_of(row):
    count = row.shape[1]
    i = lax.broadcasted_iota(jnp.int32, (count, count), 0)
    j = lax.broadcasted_iota(jnp.int32, (count, count), 1)
    return jnp.sum(jnp.where(i == j, row, 0), axis=1, keepdims=True), i, j


def dispatch_kernel(ids_ref, tokens_ref, out_ref):
    row = ids_ref[...]
    col, i, j = column_of(row)
    earlier = jnp.sum(jnp.where((col == row) & (i < j), 1, 0), axis=0, keepdims=True)
    placed = row * CAP + earlier
    slot = lax.broadcasted_iota(jnp.int32, (SLOTS, TOK), 0)
    placing = (slot == placed).astype(jnp.float32).astype(jnp.bfloat16)
    out_ref[...] = jnp.dot(
        placing, tokens_ref[...], preferred_element_type=jnp.float32
    ).astype(jnp.bfloat16)


def combine_kernel(ids_ref, back_ref, out_ref):
    row = ids_ref[...]
    col, i, j = column_of(row)
    earlier = jnp.sum(jnp.where((col == row) & (j < i), 1, 0), axis=1, keepdims=True)
    placed = col * CAP + earlier
    slot = lax.broadcasted_iota(jnp.int32, (TOK, SLOTS), 1)
    placing = (slot == placed).astype(jnp.float32).astype(jnp.bfloat16)
    out_ref[...] = jnp.dot(
        placing, back_ref[...], preferred_element_type=jnp.float32
    ).astype(jnp.bfloat16)


def gained(x_ref, k):
    rows = x_ref[k, :SLOTS, :].astype(jnp.float32)
    more = x_ref[k, SLOTS:, :].astype(jnp.float32)
    return rows, rows * (more[0:1] + more[1:2] + more[2:3]), more[3:4]


def fetched(sources, held, sems, pieces):
    depth = held.shape[1] // pieces
    copies = []
    for piece in range(pieces):
        part = pl.ds(piece * depth, depth)
        for k, source in enumerate(sources):
            copies.append(
                pltpu.make_async_copy(source.at[part], held.at[k, part], sems.at[piece, k])
            )
    for copy in copies:
        copy.start()
    return lambda piece: [c.wait() for c in copies[len(sources) * piece :][: len(sources)]]


def weighed(held, piece):
    depth = PER * FEAT
    return jnp.concatenate(
        [held[k, piece * depth : (piece + 1) * depth, :] for k in range(8)], axis=1
    )


def hidden_kernel(x_ref, *rest):
    *weights, out_ref, held, acc, made, sems, out_sems = rest
    wait = fetched(weights, held, sems, PIECES)
    squares, logit = 0.0, 0.0
    for piece in range(PIECES):
        parts = []
        for k in range(PER):
            rows, values, router = gained(x_ref, piece * PER + k)
            squares += jnp.sum(rows * rows, axis=1, keepdims=True)
            logit += jnp.sum(values * router, axis=1, keepdims=True)
            parts.append(values.astype(jnp.bfloat16))
        wait(piece)
        term = jnp.dot(
            jnp.concatenate(parts, axis=1), weighed(held, piece), preferred_element_type=jnp.float32
        )
        acc[...] = term if piece == 0 else acc[...] + term
    rstd = lax.rsqrt(squares / D + EPSILON)
    scale = rstd * jax.nn.sigmoid(logit * rstd)
    for k in range(4):
        gate = acc[:, 256 * k : 256 * k + 128] * scale
        upper = acc[:, 256 * k + 128 : 256 * k + 256] * scale
        made[:, 128 * k : 128 * k + 128] = (jax.nn.silu(gate) * upper).astype(jnp.bfloat16)
    copies = [
        pltpu.make_async_copy(made, out_ref.at[k], out_sems.at[k]) for k in range(TENSOR)
    ]
    for copy in copies:
        copy.start()
    for copy in copies:
        copy.wait()


def down_kernel(h_ref, d0, d1, d2, d3, out_ref, held, acc, sems):
    wait = fetched((d0, d1, d2, d3), held, sems, DOWN_PIECES)
    each = TENSOR // DOWN_PIECES
    for piece in range(DOWN_PIECES):
        places = range(piece * each, (piece + 1) * each)
        hidden = jnp.concatenate(
            [h for k in places for h in (h_ref[k, :, :256], h_ref[k ^ 1, :, 256:])], axis=1
        )
        wait(piece)
        slices = [held[w, 128 * k : 128 * k + 128, :] for k in places for w in range(4)]
        term = jnp.dot(
            hidden, jnp.concatenate(slices, axis=0), preferred_element_type=jnp.float32
        )
        if piece == 0:
            acc[...] = term
        elif piece < DOWN_PIECES - 1:
            acc[...] += term
        else:
            out_ref[...] = (acc[...] + term).astype(out_ref.dtype)


IN_VMEM = pl.BlockSpec(memory_space=pltpu.VMEM)
IN_HBM = pl.BlockSpec(memory_space=pl.ANY)
PARAMS = pltpu.CompilerParams(vmem_limit_bytes=VMEM)
SMALL = pltpu.CompilerParams(vmem_limit_bytes=8 * 1024 * 1024)


def left_in_hbm(arrays):
    return [pltpu.with_memory_space_constraint(a, pltpu.HBM) for a in arrays]


def hidden_copies(x, *weights):
    return pl.pallas_call(
        hidden_kernel,
        in_specs=[IN_VMEM] + [IN_HBM] * len(weights),
        out_specs=IN_HBM,
        out_shape=pltpu.HBM((TENSOR, SLOTS, 512), jnp.bfloat16),
        scratch_shapes=[
            pltpu.VMEM((8, D, 128), jnp.bfloat16),
            pltpu.VMEM((SLOTS, 1024), jnp.float32),
            pltpu.VMEM((SLOTS, 512), jnp.bfloat16),
            pltpu.SemaphoreType.DMA((PIECES, 8)),
            pltpu.SemaphoreType.DMA((TENSOR,)),
        ],
        compiler_params=PARAMS,
        cost_estimate=pl.CostEstimate(
            flops=2 * SLOTS * D * 1024,
            bytes_accessed=2 * D * (1024 + SLOTS),
            transcendentals=SLOTS * 512,
        ),
    )(x, *left_in_hbm(weights))


def spread_kernel(rows_ref, side_ref, out_ref, sems):
    copies = []
    for k in range(TENSOR):
        for n, (ref, part) in enumerate(
            ((rows_ref, pl.ds(0, SLOTS)), (side_ref, pl.ds(SLOTS, EXTRA)))
        ):
            copies.append(pltpu.make_async_copy(ref, out_ref.at[k, part], sems.at[n, k]))
    for copy in copies:
        copy.start()
    for copy in copies:
        copy.wait()


def row_copies(rows, side):
    return pl.pallas_call(
        spread_kernel,
        in_specs=[IN_VMEM, IN_VMEM],
        out_specs=IN_HBM,
        out_shape=pltpu.HBM((TENSOR, SLOTS + EXTRA, FEAT), jnp.bfloat16),
        scratch_shapes=[pltpu.SemaphoreType.DMA((2, TENSOR))],
        compiler_params=SMALL,
    )(rows, side)


def down_sums(hidden, *weights):
    return pl.pallas_call(
        down_kernel,
        in_specs=[IN_VMEM] + [IN_HBM] * 4,
        out_specs=IN_VMEM,
        out_shape=jax.ShapeDtypeStruct((SLOTS, FEAT), jnp.bfloat16),
        scratch_shapes=[
            pltpu.VMEM((4, 1024, FEAT), jnp.bfloat16),
            pltpu.VMEM((SLOTS, FEAT), jnp.float32),
            pltpu.SemaphoreType.DMA((DOWN_PIECES, 4)),
        ],
        compiler_params=PARAMS,
        cost_estimate=pl.CostEstimate(
            flops=2 * SLOTS * 4096 * FEAT,
            bytes_accessed=2 * 4096 * (FEAT + SLOTS),
            transcendentals=0,
        ),
    )(hidden, *left_in_hbm(weights))


def gathered(copies):
    return lax.all_to_all(copies, TENSOR_AXES, 0, 0, tiled=True)


def over_experts(array):
    parts = array.reshape(EXPERTS, CAP, FEAT)
    return lax.all_to_all(parts, "z", 0, 0, tiled=True).reshape(SLOTS, FEAT)


def other_core(array):
    return lax.ppermute(array, "co", [(0, 1), (1, 0)])


def across_border(array):
    return lax.ppermute(array, ("xh", "xl"), [(i, 3 - i) for i in range(4)])


def across_pair(array):
    return lax.ppermute(array, "xl", [(0, 1), (1, 0)])


def tied(*arrays):
    return lax.optimization_barrier(arrays)


def side_rows(norm_gain, router):
    high = norm_gain.astype(jnp.bfloat16)
    rest = norm_gain - high.astype(jnp.float32)
    middle = rest.astype(jnp.bfloat16)
    low = (rest - middle.astype(jnp.float32)).astype(jnp.bfloat16)
    mine = lax.axis_index("z") == jnp.arange(EXPERTS, dtype=jnp.int32)
    column = jnp.sum(jnp.where(mine[None, :], router.astype(jnp.float32), 0.0), axis=1)
    zero = jnp.zeros_like(high)
    return jnp.stack([high, middle, low, column.astype(jnp.bfloat16)] + [zero] * (EXTRA - 4))


def on_device(tokens, norm_gain, router, expert_ids, gate_proj, up_proj, down_proj):
    ids = expert_ids.reshape(1, TOK)
    gate, upper, down = gate_proj[0], up_proj[0], down_proj[0]

    outgoing = pl.pallas_call(
        dispatch_kernel, out_shape=jax.ShapeDtypeStruct((SLOTS, FEAT), jnp.bfloat16)
    )(ids, tokens)
    pair = (gate, upper)
    arrived, gate_far, token = tied(over_experts(outgoing), across_border(gate), ids)
    side = side_rows(norm_gain, router)
    down_sent = across_pair(down)

    near = [other_core(a) for a in pair]
    upper_far, down_sent, token = tied(across_border(upper), down_sent, token)
    far = (gate_far, upper_far)
    last = [other_core(a) for a in far]

    rows = gathered(row_copies(arrived, side))
    hidden = hidden_copies(rows, *pair, *near, *far, *last)

    down_far = across_border(down_sent)
    down_near, down_last = other_core(down), other_core(down_far)
    summed = down_sums(gathered(hidden), down, down_near, down_far, down_last)
    returned = over_experts(summed)
    return pl.pallas_call(
        combine_kernel,
        out_shape=jax.ShapeDtypeStruct((TOK, FEAT), jnp.bfloat16),
        compiler_params=SMALL,
    )(token, returned)


def solution(mesh):
    fine = Mesh(
        np.asarray(mesh.devices).reshape(2, 2, 16, 4, 2), ("xh", "co", "z", "y", "xl")
    )
    section, tensor = ("xh", "co"), ("y", "xl")
    in_specs = (
        P((*section, "z"), tensor),
        P(tensor),
        P(tensor, None),
        P((*section, "z"), None),
        P("z", None, (*section, *tensor)),
        P("z", None, (*section, *tensor)),
        P("z", section, tensor),
    )
    return jax.shard_map(
        on_device,
        mesh=fine,
        in_specs=in_specs,
        out_specs=P((*section, "z"), tensor),
        check_vma=False,
    )
```

```python
import jax
import jax.numpy as jnp
import numpy as np
from jax import lax
from jax.experimental import pallas as pl
from jax.experimental.pallas import tpu as pltpu
from jax.sharding import Mesh, PartitionSpec as P

D = 5120
EPSILON = 1e-05
EXPERTS = 16
CAP = 16
SLOTS = EXPERTS * CAP
TOK = 128
FEAT = 640
TENSOR = 8
EXTRA = 8
VMEM = 28 * 1024 * 1024
PIECES = 4
PER = TENSOR // PIECES
DOWN_PIECES = 4
TENSOR_AXES = ("y", "xl")


def column_of(row):
    count = row.shape[1]
    i = lax.broadcasted_iota(jnp.int32, (count, count), 0)
    j = lax.broadcasted_iota(jnp.int32, (count, count), 1)
    return jnp.sum(jnp.where(i == j, row, 0), axis=1, keepdims=True), i, j


def dispatch_kernel(ids_ref, tokens_ref, out_ref):
    row = ids_ref[...]
    col, i, j = column_of(row)
    earlier = jnp.sum(jnp.where((col == row) & (i < j), 1, 0), axis=0, keepdims=True)
    placed = row * CAP + earlier
    slot = lax.broadcasted_iota(jnp.int32, (SLOTS, TOK), 0)
    placing = (slot == placed).astype(jnp.float32).astype(jnp.bfloat16)
    out_ref[...] = jnp.dot(
        placing, tokens_ref[...], preferred_element_type=jnp.float32
    ).astype(jnp.bfloat16)


def combine_kernel(ids_ref, back_ref, out_ref):
    row = ids_ref[...]
    col, i, j = column_of(row)
    earlier = jnp.sum(jnp.where((col == row) & (j < i), 1, 0), axis=1, keepdims=True)
    placed = col * CAP + earlier
    slot = lax.broadcasted_iota(jnp.int32, (TOK, SLOTS), 1)
    placing = (slot == placed).astype(jnp.float32).astype(jnp.bfloat16)
    out_ref[...] = jnp.dot(
        placing, back_ref[...], preferred_element_type=jnp.float32
    ).astype(jnp.bfloat16)


def gained(x_ref, k):
    rows = x_ref[k, :SLOTS, :].astype(jnp.float32)
    more = x_ref[k, SLOTS:, :].astype(jnp.float32)
    return rows, rows * (more[0:1] + more[1:2] + more[2:3]), more[3:4]


def fetched(sources, held, sems, pieces):
    depth = held.shape[1] // pieces
    copies = []
    for piece in range(pieces):
        part = pl.ds(piece * depth, depth)
        for k, source in enumerate(sources):
            copies.append(
                pltpu.make_async_copy(source.at[part], held.at[k, part], sems.at[piece, k])
            )
    for copy in copies:
        copy.start()
    return lambda piece: [c.wait() for c in copies[len(sources) * piece :][: len(sources)]]


def weighed(held, piece):
    depth = PER * FEAT
    return jnp.concatenate(
        [held[k, piece * depth : (piece + 1) * depth, :] for k in range(8)], axis=1
    )


def hidden_kernel(x_ref, *rest):
    *weights, out_ref, held, acc, made, sems, out_sems = rest
    wait = fetched(weights, held, sems, PIECES)
    squares, logit = 0.0, 0.0
    for piece in range(PIECES):
        parts = []
        for k in range(PER):
            rows, values, router = gained(x_ref, piece * PER + k)
            squares += jnp.sum(rows * rows, axis=1, keepdims=True)
            logit += jnp.sum(values * router, axis=1, keepdims=True)
            parts.append(values.astype(jnp.bfloat16))
        wait(piece)
        term = jnp.dot(
            jnp.concatenate(parts, axis=1), weighed(held, piece), preferred_element_type=jnp.float32
        )
        acc[...] = term if piece == 0 else acc[...] + term
    rstd = lax.rsqrt(squares / D + EPSILON)
    scale = rstd * jax.nn.sigmoid(logit * rstd)
    for k in range(4):
        gate = acc[:, 256 * k : 256 * k + 128] * scale
        upper = acc[:, 256 * k + 128 : 256 * k + 256] * scale
        made[:, 128 * k : 128 * k + 128] = (jax.nn.silu(gate) * upper).astype(jnp.bfloat16)
    copies = [
        pltpu.make_async_copy(made, out_ref.at[k], out_sems.at[k]) for k in range(TENSOR)
    ]
    for copy in copies:
        copy.start()
    for copy in copies:
        copy.wait()


def down_kernel(h_ref, d0, d1, d2, d3, out_ref, held, acc, sems):
    wait = fetched((d0, d1, d2, d3), held, sems, DOWN_PIECES)
    each = TENSOR // DOWN_PIECES
    for piece in range(DOWN_PIECES):
        places = range(piece * each, (piece + 1) * each)
        hidden = jnp.concatenate(
            [h for k in places for h in (h_ref[k, :, :256], h_ref[k ^ 1, :, 256:])], axis=1
        )
        wait(piece)
        slices = [held[w, 128 * k : 128 * k + 128, :] for k in places for w in range(4)]
        term = jnp.dot(
            hidden, jnp.concatenate(slices, axis=0), preferred_element_type=jnp.float32
        )
        if piece == 0:
            acc[...] = term
        elif piece < DOWN_PIECES - 1:
            acc[...] += term
        else:
            out_ref[...] = (acc[...] + term).astype(out_ref.dtype)


IN_VMEM = pl.BlockSpec(memory_space=pltpu.VMEM)
IN_HBM = pl.BlockSpec(memory_space=pl.ANY)
PARAMS = pltpu.CompilerParams(vmem_limit_bytes=VMEM)
SMALL = pltpu.CompilerParams(vmem_limit_bytes=8 * 1024 * 1024)


def left_in_hbm(arrays):
    return [pltpu.with_memory_space_constraint(a, pltpu.HBM) for a in arrays]


def hidden_copies(x, *weights):
    return pl.pallas_call(
        hidden_kernel,
        in_specs=[IN_VMEM] + [IN_HBM] * len(weights),
        out_specs=IN_HBM,
        out_shape=pltpu.HBM((TENSOR, SLOTS, 512), jnp.bfloat16),
        scratch_shapes=[
            pltpu.VMEM((8, D, 128), jnp.bfloat16),
            pltpu.VMEM((SLOTS, 1024), jnp.float32),
            pltpu.VMEM((SLOTS, 512), jnp.bfloat16),
            pltpu.SemaphoreType.DMA((PIECES, 8)),
            pltpu.SemaphoreType.DMA((TENSOR,)),
        ],
        compiler_params=PARAMS,
        cost_estimate=pl.CostEstimate(
            flops=2 * SLOTS * D * 1024,
            bytes_accessed=2 * D * (1024 + SLOTS),
            transcendentals=SLOTS * 512,
        ),
    )(x, *left_in_hbm(weights))


def down_sums(hidden, *weights):
    return pl.pallas_call(
        down_kernel,
        in_specs=[IN_VMEM] + [IN_HBM] * 4,
        out_specs=IN_VMEM,
        out_shape=jax.ShapeDtypeStruct((SLOTS, FEAT), jnp.bfloat16),
        scratch_shapes=[
            pltpu.VMEM((4, 1024, FEAT), jnp.bfloat16),
            pltpu.VMEM((SLOTS, FEAT), jnp.float32),
            pltpu.SemaphoreType.DMA((DOWN_PIECES, 4)),
        ],
        compiler_params=PARAMS,
        cost_estimate=pl.CostEstimate(
            flops=2 * SLOTS * 4096 * FEAT,
            bytes_accessed=2 * 4096 * (FEAT + SLOTS),
            transcendentals=0,
        ),
    )(hidden, *left_in_hbm(weights))


def gathered(copies):
    return lax.all_to_all(copies, TENSOR_AXES, 0, 0, tiled=True)


def over_experts(array):
    parts = array.reshape(EXPERTS, CAP, FEAT)
    return lax.all_to_all(parts, "z", 0, 0, tiled=True).reshape(SLOTS, FEAT)


def other_core(array):
    return lax.ppermute(array, "co", [(0, 1), (1, 0)])


def across_border(array):
    return lax.ppermute(array, ("xh", "xl"), [(i, 3 - i) for i in range(4)])


def across_pair(array):
    return lax.ppermute(array, "xl", [(0, 1), (1, 0)])


def tied(*arrays):
    return lax.optimization_barrier(arrays)


def side_rows(norm_gain, router):
    high = norm_gain.astype(jnp.bfloat16)
    rest = norm_gain - high.astype(jnp.float32)
    middle = rest.astype(jnp.bfloat16)
    low = (rest - middle.astype(jnp.float32)).astype(jnp.bfloat16)
    mine = lax.axis_index("z") == jnp.arange(EXPERTS, dtype=jnp.int32)
    column = jnp.sum(jnp.where(mine[None, :], router.astype(jnp.float32), 0.0), axis=1)
    zero = jnp.zeros_like(high)
    return jnp.stack([high, middle, low, column.astype(jnp.bfloat16)] + [zero] * (EXTRA - 4))


def on_device(tokens, norm_gain, router, expert_ids, gate_proj, up_proj, down_proj):
    ids = expert_ids.reshape(1, TOK)
    gate, upper, down = gate_proj[0], up_proj[0], down_proj[0]

    outgoing = pl.pallas_call(
        dispatch_kernel, out_shape=jax.ShapeDtypeStruct((SLOTS, FEAT), jnp.bfloat16)
    )(ids, tokens)
    pair = (gate, upper)
    arrived, gate_far, down_sent, token = tied(
        over_experts(outgoing), across_border(gate), across_pair(down), ids
    )
    side = side_rows(norm_gain, router)

    near = [other_core(a) for a in pair]
    upper_far, down_sent, token = tied(across_border(upper), down_sent, token)
    far = (gate_far, upper_far)
    last = [other_core(a) for a in far]

    sent = jnp.concatenate([arrived, side], axis=0)
    rows = gathered(jnp.broadcast_to(sent[None], (TENSOR, *sent.shape)))
    hidden = hidden_copies(rows, *pair, *near, *far, *last)

    down_far = across_border(down_sent)
    down_near, down_last = other_core(down), other_core(down_far)
    summed = down_sums(gathered(hidden), down, down_near, down_far, down_last)
    returned = over_experts(summed)
    return pl.pallas_call(
        combine_kernel,
        out_shape=jax.ShapeDtypeStruct((TOK, FEAT), jnp.bfloat16),
        compiler_params=SMALL,
    )(token, returned)


def solution(mesh):
    fine = Mesh(
        np.asarray(mesh.devices).reshape(2, 2, 16, 4, 2), ("xh", "co", "z", "y", "xl")
    )
    section, tensor = ("xh", "co"), ("y", "xl")
    in_specs = (
        P((*section, "z"), tensor),
        P(tensor),
        P(tensor, None),
        P((*section, "z"), None),
        P("z", None, (*section, *tensor)),
        P("z", None, (*section, *tensor)),
        P("z", section, tensor),
    )
    return jax.shard_map(
        on_device,
        mesh=fine,
        in_specs=in_specs,
        out_specs=P((*section, "z"), tensor),
        check_vma=False,
    )
```
